512 devices in a mesh: dom: 64 (over z, x_hi, core), mode: 8 (over x_lo, y).
Axes of the slice: x: 4 (x_hi: 2, x_lo: 2; x = x_hi * 2 + x_lo), y: 4, z: 16, core: 2. Of those that a mesh axis runs over, the one named last changes fastest.
Arguments:
- velocity: bfloat16 [3, 256, 17, 256], P(None, 'dom'), may hold values from -6 to 6
- stress: bfloat16 [16, 6, 256, 17, 256], P('mode', None, 'dom'), may hold values from -6 to 6
- relax_time: float32 [16], replicated, may hold values from 0.2 to 2
- viscosity: float32 [16], replicated, may hold values from 0.5 to 4
- extensibility: float32 [16], replicated, may hold values from 0.05 to 0.5
Outputs:
- stress_residual: bfloat16 [16, 6, 256, 17, 256], P('mode', None, 'dom')
- stress_divergence: float32 [3, 256, 17, 256], P(None, 'dom')
The draws below stay inside these ranges and needn't reach their ends.
All inputs are finite; a program needn't handle non-finite values.
Results may differ from the reference program's by a relative error of at most 0.0074.
Values may be sent and summed in bfloat16 or wider, within the bound.
A program may use at most 128 MiB of HBM per device.

```python
import math
import jax
import jax.numpy as jnp
import numpy as np
from jax import lax

MODES = 16
NR = 17
NT = 256
NZ = 256


def steps_of(rng, shape, cuts, least, largest):
    def one(position, parts):
        heights = jax.random.uniform(jax.random.fold_in(jax.random.fold_in(rng, 6), position), (parts,), jnp.float32, least / len(cuts), largest / len(cuts))
        return jnp.repeat(jnp.exp(heights), shape[position] // parts).reshape((-1,) + (1,) * (len(shape) - position - 1))

    gain = one(*cuts[0])
    for cut in cuts[1:]:
        gain = gain * one(*cut)
    return gain


def noise(key, dims, scale, limit, split=(), kind=jnp.bfloat16):
    drawn = scale * jax.random.normal(key, dims, jnp.float32)
    if split:
        drawn = drawn * steps_of(key, dims, split, -0.22, 0.18)
    return jnp.clip(drawn, -limit, limit).astype(kind)


def setup_inputs(seed: int = 0) -> dict:
    keys = jax.random.split(jax.random.key(seed), 6)
    velocity = noise(keys[0], (3, NZ, NR, NT), 1.0, 6.0, ((1, 64),))
    stress = noise(keys[1], (MODES, 6, NZ, NR, NT), 1.0, 6.0, ((0, 8), (2, 64)))
    relax_time = jnp.clip(jnp.exp(jax.random.uniform(keys[2], (MODES,), jnp.float32, math.log(0.2), math.log(2.0))), 0.2, 2.0)
    viscosity = jnp.clip(jnp.exp(jax.random.uniform(keys[3], (MODES,), jnp.float32, math.log(0.5), math.log(4.0))), 0.5, 4.0)
    extensibility = jnp.clip(jax.random.uniform(keys[4], (MODES,), jnp.float32, 0.05, 0.5), 0.05, 0.5)
    return dict(velocity=velocity, stress=stress, relax_time=relax_time, viscosity=viscosity, extensibility=extensibility)


component_slot = ((0, 3, 4), (3, 1, 5), (4, 5, 2))
component_pairs = ((0, 0), (1, 1), (2, 2), (0, 1), (0, 2), (1, 2))

def gauss_tables():
    gauss_points = np.array([0.5 - 0.5 * np.sqrt(0.6), 0.5, 0.5 + 0.5 * np.sqrt(0.6)])
    line_weight = np.array([5.0, 8.0, 5.0]) / 18.0
    basis_value = np.stack([2.0 * gauss_points * gauss_points - 3.0 * gauss_points + 1.0, 4.0 * gauss_points * (1.0 - gauss_points), 2.0 * gauss_points * gauss_points - gauss_points], axis=1)
    basis_slope = np.stack([4.0 * gauss_points - 3.0, 4.0 - 8.0 * gauss_points, 4.0 * gauss_points - 1.0], axis=1)

    def product(first_table, second_table, third_table):
        joined = first_table[:, None, None, :, None, None] * second_table[None, :, None, None, :, None] * third_table[None, None, :, None, None, :]
        return joined.reshape(27, 27)
    forward = np.concatenate([product(basis_value, basis_value, basis_value), product(basis_slope, basis_value, basis_value), product(basis_value, basis_slope, basis_value), product(basis_value, basis_value, basis_slope)], axis=0)
    volume_weight = (line_weight[:, None, None] * line_weight[None, :, None] * line_weight[None, None, :]).reshape(27)
    testing = (forward * np.tile(volume_weight, 4)[:, None]).T
    return (jnp.asarray(forward, dtype=jnp.bfloat16), jnp.asarray(testing, dtype=jnp.bfloat16))

def node_mass(plane_count, cycle_nodes, around_nodes, first_mass):
    plane_ids = jnp.arange(plane_count, dtype=jnp.int32)
    cycle_ids = jnp.arange(cycle_nodes, dtype=jnp.int32)
    around_ids = jnp.arange(around_nodes, dtype=jnp.int32)
    plane_mass = jnp.where(plane_ids % 2 == 1, 2.0 / 3.0, jnp.where(plane_ids == 0, first_mass, 1.0 / 3.0)).astype(jnp.float32)
    cycle_mass = jnp.where(cycle_ids % 2 == 1, 2.0 / 3.0, jnp.where((cycle_ids == 0) | (cycle_ids == cycle_nodes - 1), 1.0 / 6.0, 1.0 / 3.0)).astype(jnp.float32)
    around_mass = jnp.where(around_ids % 2 == 1, 2.0 / 3.0, 1.0 / 3.0).astype(jnp.float32)
    return plane_mass[:, None, None] * cycle_mass[None, :, None] * around_mass[None, None, :]

def element_tiles(plane_slab, cycle_count):
    channels = plane_slab.shape[0]
    pieces = []
    for plane_shift in range(3):
        for cycle_shift in range(3):
            radial = plane_slab[:, plane_shift, cycle_shift:cycle_shift + 2 * cycle_count - 1:2]
            even_nodes = radial[:, :, 0::2]
            odd_nodes = radial[:, :, 1::2]
            pieces.extend([even_nodes, odd_nodes, jnp.roll(even_nodes, -1, axis=2)])
    stacked = jnp.stack(pieces, axis=0)
    return stacked.reshape(27, channels * stacked.shape[2] * stacked.shape[3])

def assemble_layer(contrib, channels, cycle_count):
    beside_all = contrib.shape[1] // (channels * cycle_count)
    pieces = contrib.reshape(27, channels, cycle_count, beside_all)
    planes_out = []
    for plane_shift in range(3):
        cycle_parts = []
        for cycle_shift in range(3):
            corner = 9 * plane_shift + 3 * cycle_shift
            even_nodes = pieces[corner] + jnp.roll(pieces[corner + 2], 1, axis=2)
            cycle_parts.append(jnp.stack([even_nodes, pieces[corner + 1]], axis=3).reshape(channels, cycle_count, 2 * beside_all))
        even_cycles = jnp.pad(cycle_parts[0], ((0, 0), (0, 1), (0, 0))) + jnp.pad(cycle_parts[2], ((0, 0), (1, 0), (0, 0)))
        merged = jnp.stack([even_cycles[:, :cycle_count], cycle_parts[1]], axis=2).reshape(channels, 2 * cycle_count, 2 * beside_all)
        planes_out.append(jnp.concatenate([merged, even_cycles[:, cycle_count:]], axis=1))
    return jnp.stack(planes_out, axis=1)

def velocity_points(plane_slab, forward, cycle_count):
    velocity_tiles = element_tiles(plane_slab, cycle_count)
    return jnp.dot(forward, velocity_tiles, preferred_element_type=jnp.float32).astype(jnp.bfloat16)

def gradient_contrib(layer_points, testing, cycle_count):
    at_points = layer_points.reshape(4, 27, 3, -1)
    gradient = jnp.transpose(at_points[1:], (1, 2, 0, 3)).reshape(27, -1)
    contrib = jnp.dot(testing[:, :27], gradient, preferred_element_type=jnp.float32)
    return assemble_layer(contrib, 9, cycle_count)

def gradient_pass(source, layer_count, forward, testing, cycle_count):
    initial = jnp.zeros((9, source.shape[2], source.shape[3]), jnp.float32)

    def gradient_step(pending, layer_index):
        plane_slab = lax.dynamic_slice_in_dim(source, 2 * layer_index, 3, axis=1)
        layer_points = velocity_points(plane_slab, forward, cycle_count)
        layer_part = gradient_contrib(layer_points, testing, cycle_count)
        finished = jnp.stack([pending + layer_part[:, 0], layer_part[:, 1]], axis=1)
        return (layer_part[:, 2], (finished, layer_points))
    return lax.scan(gradient_step, initial, jnp.arange(layer_count, dtype=jnp.int32))

def join_planes(finished, plane_axis):
    moved = jnp.moveaxis(finished, 0, plane_axis)
    new_shape = moved.shape[:plane_axis] + (moved.shape[plane_axis] * 2,) + moved.shape[plane_axis + 2:]
    return moved.reshape(new_shape)

def layer_state(layer_points, gradient_slab, forward, cycle_count):
    at_points = layer_points.astype(jnp.float32).reshape(4, 27, 3, -1)
    flow_velocity = at_points[0]
    gradient_tiles = element_tiles(gradient_slab, cycle_count)
    projected = jnp.dot(forward[:27], gradient_tiles, preferred_element_type=jnp.float32).reshape(27, 9, -1)
    upwind = 0.5 / (1.0 + jnp.sqrt(lax.optimization_barrier(jnp.sum(flow_velocity * flow_velocity, axis=1))))
    return (at_points, projected, upwind)

def mode_layer(layer_data, stress_slab, mode_relax, mode_viscosity, mode_extension, forward, testing, cycle_count):
    at_points, projected, upwind = layer_data
    flow_velocity = at_points[0]
    stress_points = jnp.dot(forward, element_tiles(stress_slab, cycle_count), preferred_element_type=jnp.float32).reshape(4, 27, 6, -1)

    def stress_entry(block_index, left_index, right_index):
        return stress_points[block_index, :, component_slot[left_index][right_index]]

    def gradient_entry(left_index, right_index):
        return projected[:, 3 * left_index + right_index]
    trace_sum = stress_entry(0, 0, 0) + stress_entry(0, 1, 1) + stress_entry(0, 2, 2)
    factor = 1.0 + mode_extension * mode_relax / mode_viscosity * trace_sum
    residual_rows = []
    for left_index, right_index in component_pairs:
        advect = flow_velocity[:, 0] * stress_entry(1, left_index, right_index) + flow_velocity[:, 1] * stress_entry(2, left_index, right_index) + flow_velocity[:, 2] * stress_entry(3, left_index, right_index)
        stretch = jnp.zeros_like(advect)
        for inner_index in range(3):
            stretch = stretch + gradient_entry(left_index, inner_index) * stress_entry(0, inner_index, right_index) + stress_entry(0, left_index, inner_index) * gradient_entry(right_index, inner_index)
        residual_rows.append(factor * stress_entry(0, left_index, right_index) + mode_relax * (advect - stretch) - mode_viscosity * (gradient_entry(left_index, right_index) + gradient_entry(right_index, left_index)))
    residual = jnp.stack(residual_rows, axis=1)
    weighted = upwind[:, None, :] * residual
    test_flux = jnp.stack([residual, flow_velocity[:, 0:1] * weighted, flow_velocity[:, 1:2] * weighted, flow_velocity[:, 2:3] * weighted], axis=0).reshape(108, -1).astype(jnp.bfloat16)
    stress_part = assemble_layer(jnp.dot(testing, test_flux, preferred_element_type=jnp.float32), 6, cycle_count)
    divergence_flux = jnp.stack([jnp.stack([stress_entry(0, left_index, right_index) for left_index in range(3)], axis=1) for right_index in range(3)], axis=0).reshape(81, -1).astype(jnp.bfloat16)
    divergence_part = assemble_layer(jnp.dot(testing[:, 27:], divergence_flux, preferred_element_type=jnp.float32), 3, cycle_count)
    return (stress_part, divergence_part)

def devss_layer(layer_data, devss_weight, testing, cycle_count):
    at_points, projected, upwind = layer_data
    columns = []
    for right_index in range(3):
        rows_list = []
        for left_index in range(3):
            rows_list.append(devss_weight * (at_points[1 + right_index, :, left_index] + at_points[1 + left_index, :, right_index] - projected[:, 3 * left_index + right_index] - projected[:, 3 * right_index + left_index]))
        columns.append(jnp.stack(rows_list, axis=1))
    devss_flux = jnp.stack(columns, axis=0).reshape(81, -1).astype(jnp.bfloat16)
    return assemble_layer(jnp.dot(testing[:, 27:], devss_flux, preferred_element_type=jnp.float32), 3, cycle_count)

def reference(velocity, stress, relax_time, viscosity, extensibility):
    forward, testing = gauss_tables()
    cycle_nodes = velocity.shape[2]
    around_nodes = velocity.shape[3]
    cycle_count = (cycle_nodes - 1) // 2
    planes = velocity.shape[1]
    layers = planes // 2
    velocity_full = jnp.concatenate([velocity, jnp.zeros_like(velocity[:, :1])], axis=1)
    stress_full = jnp.concatenate([stress, jnp.zeros_like(stress[:, :, :1])], axis=2)
    lumped_mass = node_mass(planes, cycle_nodes, around_nodes, 1.0 / 6.0)
    leftover, (finished, unused_points) = gradient_pass(velocity_full, layers, forward, testing, cycle_count)
    partial_planes = join_planes(finished, 1)
    projected_nodes = (partial_planes / lumped_mass).astype(jnp.bfloat16)
    projected = jnp.concatenate([projected_nodes, jnp.zeros_like(projected_nodes[:, :1])], axis=1)
    devss_weight = jnp.mean(viscosity)
    modes_total = stress.shape[0]

    def stress_step(pending, layer_index):
        pending_stress, pending_divergence = pending
        plane_slab = lax.dynamic_slice_in_dim(velocity_full, 2 * layer_index, 3, axis=1)
        layer_points = velocity_points(plane_slab, forward, cycle_count)
        gradient_slab = lax.dynamic_slice_in_dim(projected, 2 * layer_index, 3, axis=1)
        layer_data = layer_state(layer_points, gradient_slab, forward, cycle_count)
        stress_slabs = lax.dynamic_slice_in_dim(stress_full, 2 * layer_index, 3, axis=2)

        def single_mode(mode_inputs):
            return mode_layer(layer_data, mode_inputs[0], mode_inputs[1], mode_inputs[2], mode_inputs[3], forward, testing, cycle_count)
        stress_parts, divergence_parts = lax.map(single_mode, (stress_slabs, relax_time, viscosity, extensibility))
        divergence_total = lax.optimization_barrier(jnp.sum(divergence_parts, axis=0)) + devss_layer(layer_data, devss_weight, testing, cycle_count)
        done_stress = jnp.stack([pending_stress + stress_parts[:, :, 0], stress_parts[:, :, 1]], axis=2).astype(jnp.bfloat16)
        done_divergence = jnp.stack([pending_divergence + divergence_total[:, 0], divergence_total[:, 1]], axis=1)
        return ((stress_parts[:, :, 2], divergence_total[:, 2]), (done_stress, done_divergence))
    initial = (jnp.zeros((modes_total, 6, cycle_nodes, around_nodes), jnp.float32), jnp.zeros((3, cycle_nodes, around_nodes), jnp.float32))
    leftover_sums, (done_stress, done_divergence) = lax.scan(stress_step, initial, jnp.arange(layers, dtype=jnp.int32))
    return (join_planes(done_stress, 2), join_planes(done_divergence, 1))
```

```python
import functools

import jax
import jax.numpy as jnp
import ml_dtypes
import numpy as np
from jax import lax
from jax.experimental import pallas as pl
from jax.experimental.pallas import tpu as pltpu
from jax.sharding import PartitionSpec as P

F32 = jnp.float32
BF16 = jnp.bfloat16
MESH = pl.DeviceIdType.MESH
SLOT = ((0, 3, 4), (3, 1, 5), (4, 5, 2))
NODES = 17
ROWS = 24
WINDOW = 256
POINTS = 224
LANES = 128


def gauss_tables():
    s = np.array([0.5 - 0.5 * np.sqrt(0.6), 0.5, 0.5 + 0.5 * np.sqrt(0.6)])
    weight = np.array([5.0, 8.0, 5.0]) / 18.0
    value = np.stack([2.0 * s * s - 3.0 * s + 1.0, 4.0 * s * (1.0 - s), 2.0 * s * s - s], axis=1)
    slope = np.stack([4.0 * s - 3.0, 4.0 - 8.0 * s, 4.0 * s - 1.0], axis=1)

    def product(first, second, third):
        joined = (
            first[:, None, None, :, None, None]
            * second[None, :, None, None, :, None]
            * third[None, None, :, None, None, :]
        )
        return joined.reshape(27, 27)

    forward = np.concatenate(
        [
            product(value, value, value),
            product(slope, value, value),
            product(value, slope, value),
            product(value, value, slope),
        ],
        axis=0,
    )
    volume = (weight[:, None, None] * weight[None, :, None] * weight[None, None, :]).reshape(27)
    testing = (forward * np.tile(volume, 4)[:, None]).T
    return forward.astype(ml_dtypes.bfloat16), testing.astype(ml_dtypes.bfloat16)


def column_tables():
    forward, testing = (np.asarray(t, np.float32) for t in gauss_tables())
    ahead = np.zeros((4, POINTS, WINDOW), np.float32)
    back = np.zeros((WINDOW, 4, 256), np.float32)
    for f in range((NODES - 1) // 2):
        for n in range(27):
            a, b, c = n // 9, (n // 3) % 3, n % 3
            node = 3 * ROWS * a + ROWS * c + 2 * f + b
            for d in range(4):
                rows = slice(27 * d, 27 * d + 27)
                ahead[d, 27 * f : 27 * f + 27, node] = forward[rows, n]
                back[node, d, 27 * f : 27 * f + 27] = testing[n, rows]
    back = back[: 9 * ROWS].reshape(9 * ROWS, 4 * 256)
    return ahead.astype(ml_dtypes.bfloat16), back.astype(ml_dtypes.bfloat16)


def order_tables():
    split = np.zeros((2 * LANES, 3 * LANES), np.float32)
    for g in range(LANES):
        split[2 * g, g] = 1.0
        split[2 * g + 1, LANES + g] = 1.0
        split[(2 * g + 2) % (2 * LANES), 2 * LANES + g] = 1.0
    merge = split[:, : 2 * LANES].T.copy()
    return split.astype(ml_dtypes.bfloat16), merge.astype(ml_dtypes.bfloat16)


def inverse_mass():
    r = np.arange(ROWS)
    mr = np.where(r % 2 == 1, 2.0 / 3.0, np.where((r == 0) | (r == NODES - 1), 1.0 / 6.0, 1.0 / 3.0))
    both = np.stack([3.0 / mr, 1.5 / mr])
    return np.ascontiguousarray(np.broadcast_to(both[:, :, None], (2, ROWS, LANES))).astype(np.float32)


def dot(x, y):
    return jnp.dot(x, y, preferred_element_type=F32)


def padded(x):
    return jnp.concatenate([x.astype(F32), jnp.zeros((ROWS - NODES, x.shape[1]), F32)], axis=0)


def stacked(parts, height):
    rows = sum(p.shape[0] for p in parts)
    if rows < height:
        parts = parts + [jnp.zeros((height - rows, parts[0].shape[1]), F32)]
    return jnp.concatenate(parts, axis=0).astype(BF16)


def block(column, a, c):
    start = 3 * ROWS * a + ROWS * c
    return column[start : start + ROWS]


def around(column, a):
    even = block(column, a, 0) + pltpu.roll(block(column, a, 2), 1, axis=1)
    return even, block(column, a, 1)


def kernel(
    doms,
    modes,
    velocity,
    stress,
    relax,
    viscosity,
    extension,
    ahead,
    back,
    split,
    merge,
    inv_mass,
    out_stress,
    out_div,
    vel_up,
    vel_dn,
    str_up,
    s_nodes,
    v_nodes,
    p_nodes,
    t_points,
    flux,
    dflux,
    derivs,
    grads,
    flow,
    winds,
    g_points,
    sums,
    devss,
    shares,
    rs_send,
    rs_recv,
    ag_buf,
    cup_send,
    cup_recv,
    top_send,
    top_recv,
    rows_s,
    halo_send,
    halo_recv,
    rs_ssem,
    rs_rsem,
    ag_ssem,
    ag_rsem,
    top_ssem,
    top_rsem,
):
    dom = lax.axis_index("dom")
    mode = lax.axis_index("mode")
    has_below = dom > 0
    has_above = dom < doms - 1
    below = (jnp.maximum(dom - 1, 0), mode)
    above = (jnp.minimum(dom + 1, doms - 1), mode)

    barrier = pltpu.get_barrier_semaphore()
    for off in range(1, modes):
        peer = lax.rem(mode + off, modes)
        pl.semaphore_signal(barrier, inc=1, device_id=(dom, peer), device_id_type=MESH)

    @pl.when(has_below)
    def _():
        pl.semaphore_signal(barrier, inc=1, device_id=below, device_id_type=MESH)

    @pl.when(has_above)
    def _():
        pl.semaphore_signal(barrier, inc=1, device_id=above, device_id_type=MESH)

    def remote(src, dst, send, recv, target):
        return pltpu.make_async_remote_copy(
            src_ref=src,
            dst_ref=dst,
            send_sem=send,
            recv_sem=recv,
            device_id=target,
            device_id_type=MESH,
        )

    down_stress = remote(stress.at[:, :, 0], str_up, halo_send.at[0], halo_recv.at[0], below)
    down_velocity = remote(velocity.at[:, 0:3], vel_up, halo_send.at[1], halo_recv.at[1], below)
    up_velocity = remote(velocity.at[:, 2:4], vel_dn, halo_send.at[2], halo_recv.at[2], above)
    up_share = remote(cup_send, cup_recv, halo_send.at[3], halo_recv.at[3], above)

    @pl.when(jnp.logical_not(has_above))
    def _():
        vel_up[...] = jnp.zeros_like(vel_up)
        str_up[...] = jnp.zeros_like(str_up)

    @pl.when(jnp.logical_not(has_below))
    def _():
        vel_dn[...] = jnp.zeros_like(vel_dn)
        cup_recv[...] = jnp.zeros_like(cup_recv)
        top_recv[...] = jnp.zeros_like(top_recv)

    others = modes - 1 + has_below.astype(jnp.int32) + has_above.astype(jnp.int32)
    pl.semaphore_wait(barrier, others)

    @pl.when(has_below)
    def _():
        down_velocity.start()
        down_stress.start()

    @pl.when(has_above)
    def _():
        up_velocity.start()

    def laid_out(planes):
        rows = len(planes) * ROWS
        height = -(-rows // 16) * 16
        spread = dot(stacked([padded(p) for p in planes], height), split[...])
        result = []
        for k in range(len(planes)):
            here = spread[k * ROWS : (k + 1) * ROWS]
            result.append([here[:, LANES * c : LANES * (c + 1)] for c in range(3)])
        return result

    PAIR = 6 * ROWS

    def lay_stress(k, _):
        planes = laid_out([stress[k // 2, 3 * (k % 2) + c, p] for c in range(3) for p in range(4)])
        for c in range(3):
            for pair in range(2):
                two = planes[4 * c + 2 * pair] + planes[4 * c + 2 * pair + 1]
                s_nodes[3 * k + c, (pair + 1) * PAIR : (pair + 2) * PAIR] = stacked(two, PAIR)
            s_nodes[3 * k + c, 0:PAIR] = jnp.zeros((PAIR, LANES), BF16)
            s_nodes[3 * k + c, 3 * PAIR :] = jnp.zeros((WINDOW - PAIR, LANES), BF16)
        return 0

    lax.fori_loop(0, 4, lay_stress, 0)
    for d in range(4):
        flux[256 * d + POINTS : 256 * (d + 1)] = jnp.zeros((256 - POINTS, 6 * LANES), BF16)
    for d in range(3):
        dflux[256 * d + POINTS : 256 * (d + 1)] = jnp.zeros((256 - POINTS, 3 * LANES), BF16)

    def stress_window(m, layer):
        start = (layer + 1) * PAIR
        return jnp.concatenate(
            [s_nodes[6 * m + c, start : start + WINDOW] for c in range(6)], axis=1
        )

    def column(c):
        return slice(LANES * c, LANES * (c + 1))

    def divergence_of(layer):
        for m in range(2):
            t_points[m] = dot(ahead[0], stress_window(m, layer))
        for c in range(6):
            both = (t_points[0, :, column(c)] + t_points[1, :, column(c)]).astype(BF16)
            for j in range(3):
                for i in range(3):
                    if SLOT[i][j] == c:
                        dflux[256 * j : 256 * j + POINTS, column(i)] = both
        return dot(back[:, 256:], dflux[...])

    upper = divergence_of(1)
    for i in range(3):
        even, odd = around(upper[:, column(i)], 2)
        cup_send[i] = stacked([even, odd], 2 * ROWS)

    @pl.when(has_above)
    def _():
        up_share.start()

    under = divergence_of(-1)
    inside = jnp.where(has_below, 1.0, 0.0).astype(F32)
    for i in range(3):
        even, odd = around(under[:, column(i)], 2)
        shares[0, i] = even * inside
        shares[1, i] = odd * inside
    middle = divergence_of(0)
    for i in range(3):
        for a in range(3):
            even, odd = around(middle[:, column(i)], a)
            if a == 0:
                even, odd = even + shares[0, i], odd + shares[1, i]
            shares[2 * a, i] = even
            shares[2 * a + 1, i] = odd

    for i in range(3):
        planes = laid_out([velocity[i, p] for p in range(4)])
        for pair in range(2):
            two = planes[2 * pair] + planes[2 * pair + 1]
            v_nodes[i, (pair + 1) * PAIR : (pair + 2) * PAIR] = stacked(two, PAIR)

    for layer in range(2):
        start = (layer + 1) * PAIR
        if layer == 1:

            @pl.when(has_above)
            def _():
                down_velocity.wait_recv()

            @pl.when(has_below)
            def _():
                up_velocity.wait_recv()

            for i in range(3):
                planes = laid_out([vel_dn[i, 0], vel_dn[i, 1]] + [vel_up[i, p] for p in range(3)])
                v_nodes[i, 0:PAIR] = stacked(planes[0] + planes[1], PAIR)
                v_nodes[i, 3 * PAIR : 4 * PAIR] = stacked(planes[2] + planes[3], PAIR)
                v_nodes[i, 4 * PAIR :] = stacked(planes[4], WINDOW - PAIR)
        nodes = jnp.concatenate([v_nodes[i, start : start + WINDOW] for i in range(3)], axis=1)
        at = dot(ahead[0], nodes).astype(BF16).astype(F32)
        u = [at[:, column(i)] for i in range(3)]
        upwind = 0.5 / (1.0 + jnp.sqrt(u[0] * u[0] + u[1] * u[1] + u[2] * u[2]))
        for i in range(3):
            flow[layer, i] = u[i]
            winds[layer, i] = (upwind * u[i]).astype(BF16)

    def gradient_layer(layer, _):
        start = pl.multiple_of(layer * PAIR, 16)
        nodes = jnp.concatenate([v_nodes[i, pl.ds(start, WINDOW)] for i in range(3)], axis=1)
        for j in range(3):
            at = dot(ahead[1 + j], nodes)
            derivs[layer, j] = stacked([at], 256)
            grads[layer, j] = dot(back[:, 0:256], derivs[layer, j])
        return 0

    lax.fori_loop(0, 4, gradient_layer, 0)

    first_mass = jnp.where(has_below, 3.0, 6.0).astype(F32)
    last_mass = jnp.where(has_above, 3.0, 0.0).astype(F32)
    plane_mass = [first_mass, 1.5, 3.0, 1.5, last_mass]
    sources = [[(0, 2), (1, 0)], [(1, 1)], [(1, 2), (2, 0)], [(2, 1)], [(2, 2), (3, 0)]]

    def project(j, _):
        for i in range(3):
            blocks = []
            for p in range(5):
                total = [0.0, 0.0, 0.0]
                for layer, a in sources[p]:
                    for c in range(3):
                        start = 3 * ROWS * a + ROWS * c
                        part = grads[layer, j, start : start + ROWS, column(i)]
                        if layer == 0:
                            part = part * inside
                        total[c] = total[c] + part
                even = total[0] + pltpu.roll(total[2], 1, axis=1)
                even = even * (inv_mass[0] * plane_mass[p])
                odd = total[1] * (inv_mass[1] * plane_mass[p])
                blocks.append([even, odd, pltpu.roll(even, LANES - 1, axis=1)])
            p_nodes[3 * i + j, 0:PAIR] = stacked(blocks[0] + blocks[1], PAIR)
            p_nodes[3 * i + j, PAIR : 2 * PAIR] = stacked(blocks[2] + blocks[3], PAIR)
            p_nodes[3 * i + j, 2 * PAIR :] = stacked(blocks[4], WINDOW - PAIR)
        return 0

    lax.fori_loop(0, 3, project, 0)

    for layer in range(2):
        for i in range(3):
            nodes = jnp.concatenate(
                [p_nodes[3 * i + j, layer * PAIR : layer * PAIR + WINDOW] for j in range(3)], axis=1
            )
            here = dot(ahead[0], nodes)
            for j in range(3):
                g_points[layer, 3 * i + j] = here[:, column(j)]

    @pl.when(has_above)
    def _():
        down_stress.wait_recv()

    for k in range(4):
        planes = laid_out([str_up[k // 2, 3 * (k % 2) + c] for c in range(3)])
        for c in range(3):
            s_nodes[3 * k + c, 3 * PAIR :] = stacked(planes[c], WINDOW - PAIR)

    upper = divergence_of(1)

    @pl.when(has_below)
    def _():
        up_share.wait_recv()

    for i in range(3):
        from_below = cup_recv[i].astype(F32)
        shares[0, i] = shares[0, i] + from_below[0:ROWS]
        shares[1, i] = shares[1, i] + from_below[ROWS:]
        for a in range(2):
            even, odd = around(upper[:, column(i)], a)
            if a == 0:
                even, odd = even + shares[4, i], odd + shares[5, i]
            shares[4 + 2 * a, i] = even
            shares[5 + 2 * a, i] = odd
    for k in range(8):
        rs_send[k] = stacked([shares[k, i] for i in range(3)], 80)

    def share_copy(off):
        peer = lax.rem(mode + off, modes)
        return remote(
            rs_send.at[peer], rs_recv.at[off], rs_ssem.at[off], rs_rsem.at[off], (dom, peer)
        )

    for off in range(1, modes):
        share_copy(off).start()

    def residual_of(layer, m):
        lam = jnp.full((16, LANES), relax[2 * mode + m], F32)
        eta = jnp.full((16, LANES), viscosity[2 * mode + m], F32)
        eps = jnp.full((16, LANES), extension[2 * mode + m], F32)
        half = 0.5 / lam
        slope = 0.5 * eps / eta
        kappa = eta / lam
        nodes = stress_window(m, layer)
        for d in range(4):
            t_points[d] = dot(ahead[d], nodes)

        def chunk(start):
            rows = pl.ds(start, 16)
            t = [t_points[0, rows, column(c)] for c in range(6)]
            g = [[g_points[layer, 3 * i + j, rows] for j in range(3)] for i in range(3)]
            u = [flow[layer, i, rows] for i in range(3)]
            y = half + slope * (t[0] + t[1] + t[2])
            shift = (y * kappa) * 2.0
            tt = [t[0] + kappa, t[1] + kappa, t[2] + kappa] + t[3:]
            h = [g[k][k] - y for k in range(3)]

            def entry(i, j):
                return tt[SLOT[i][j]]

            result = []
            for c, (i, j) in enumerate(((0, 0), (1, 1), (2, 2), (0, 1), (0, 2), (1, 2))):
                value = u[0] * t_points[1, rows, column(c)]
                value = value + u[1] * t_points[2, rows, column(c)]
                value = value + u[2] * t_points[3, rows, column(c)]
                if i == j:
                    k, l = (i + 1) % 3, (i + 2) % 3
                    part = h[i] * entry(i, i) + g[i][k] * entry(k, i) + g[i][l] * entry(l, i)
                    value = value - (part + part) - shift
                else:
                    k = 3 - i - j
                    part = (h[i] + h[j]) * entry(i, j)
                    part = part + g[i][j] * entry(j, j) + g[i][k] * entry(k, j)
                    part = part + g[j][i] * entry(i, i) + g[j][k] * entry(k, i)
                    value = value - part
                result.append(value)
            for c in range(6):
                rounded = result[c].astype(BF16)
                flux[rows, column(c)] = rounded
                for j in range(3):
                    place = pl.ds(256 * (1 + j) + start, 16)
                    flux[place, column(c)] = rounded * winds[layer, j, rows]

        def two_chunks(k, _):
            start = pl.multiple_of(32 * k, 32)
            chunk(start)
            chunk(start + 16)
            return 0

        lax.fori_loop(0, POINTS // 32, two_chunks, 0)
        sums[2 * layer + m] = dot(back[...], flux[...])

    weight = viscosity[0]
    for k in range(1, 2 * modes):
        weight = weight + viscosity[k]
    weight = weight * (1.0 / (2 * modes))

    def devss_of(layer):
        for i in range(3):
            for j in range(i, 3):
                d_ij = derivs[layer + 1, j, 0:POINTS, column(i)].astype(F32)
                d_ji = derivs[layer + 1, i, 0:POINTS, column(j)].astype(F32)
                excess = d_ij + d_ji - g_points[layer, 3 * i + j] - g_points[layer, 3 * j + i]
                value = (weight * excess).astype(BF16)
                dflux[256 * j : 256 * j + POINTS, column(i)] = value
                if i != j:
                    dflux[256 * i : 256 * i + POINTS, column(j)] = value
        devss[layer] = dot(back[:, 256:], dflux[...])

    def top_copy(k, first, count):
        part = pl.ds(first, count)
        return remote(top_send.at[part], top_recv.at[part], top_ssem.at[k], top_rsem.at[k], above)

    tops = [top_copy(0, 0, 6), top_copy(1, 6, 6), top_copy(2, 12, 3)]

    def start_top(k):
        @pl.when(has_above)
        def _():
            tops[k].start()

    for m in range(2):
        residual_of(1, m)
        for c in range(6):
            even, odd = around(sums[2 + m, :, column(c)], 2)
            top_send[6 * m + c] = stacked([even, odd], 2 * ROWS)
        start_top(m)
    devss_of(1)
    for i in range(3):
        even, odd = around(devss[1, :, column(i)], 2)
        top_send[12 + i] = stacked([even, odd], 2 * ROWS)
    start_top(2)

    total = jnp.concatenate([shares[mode, i] for i in range(3)] + [jnp.zeros((8, LANES), F32)], axis=0)
    for off in range(1, modes):
        share_copy(off).wait_recv()
        total = total + rs_recv[off].astype(F32)
    ag_buf[mode] = total.astype(BF16)

    def whole_copy(off, slot):
        peer = lax.rem(mode + off, modes)
        return remote(
            ag_buf.at[slot], ag_buf.at[slot], ag_ssem.at[off], ag_rsem.at[off], (dom, peer)
        )

    for off in range(1, modes):
        whole_copy(off, mode).start()

    for m in range(2):
        residual_of(0, m)
    devss_of(0)

    for off in range(1, modes):
        whole_copy(off, lax.rem(mode + modes - off, modes)).wait_recv()

    @pl.when(has_below)
    def _():
        for k in range(3):
            tops[k].wait_recv()

    place = [[(0, 0)], [(0, 1)], [(0, 2), (1, 0)], [(1, 1)]]

    def finish(k, _):
        m, c0 = k // 2, 3 * (k % 2)
        lam = relax[2 * mode + m]
        pieces = []
        for c in range(3):
            for p in range(4):
                even, odd = 0.0, 0.0
                for layer, a in place[p]:
                    start = 3 * ROWS * a
                    cols = pl.ds(pl.multiple_of((c0 + c) * LANES, LANES), LANES)
                    first = sums[2 * layer + m, start : start + ROWS, cols]
                    second = sums[2 * layer + m, start + ROWS : start + 2 * ROWS, cols]
                    third = sums[2 * layer + m, start + 2 * ROWS : start + 3 * ROWS, cols]
                    even = even + (first + pltpu.roll(third, 1, axis=1))
                    odd = odd + second
                if p == 0:
                    from_below = top_recv[6 * m + c0 + c].astype(F32)
                    even = even + from_below[0:ROWS]
                    odd = odd + from_below[ROWS:]
                pieces.append(jnp.concatenate([even * lam, odd * lam], axis=1))
        merged = dot(stacked(pieces, 12 * ROWS), merge[...]).astype(BF16)
        rows_s[...] = merged.astype(F32)
        for c in range(3):
            for p in range(4):
                start = (4 * c + p) * ROWS
                out_stress[m, c0 + c, p] = rows_s[start : start + NODES].astype(BF16)
        return 0

    lax.fori_loop(0, 4, finish, 0)

    high, low = [], []
    for i in range(3):
        for p in range(4):
            even = ag_buf[2 * p].astype(F32)[ROWS * i : ROWS * (i + 1)]
            odd = ag_buf[2 * p + 1].astype(F32)[ROWS * i : ROWS * (i + 1)]
            for layer, a in place[p]:
                more_even, more_odd = around(devss[layer, :, column(i)], a)
                even, odd = even + more_even, odd + more_odd
            if p == 0:
                from_below = top_recv[12 + i].astype(F32)
                even = even + from_below[0:ROWS]
                odd = odd + from_below[ROWS:]
            both = jnp.concatenate([even, odd], axis=1)
            rounded = both.astype(BF16).astype(F32)
            high.append(rounded)
            low.append(both - rounded)
    rows_s[...] = dot(stacked(high, 12 * ROWS), merge[...]) + dot(
        stacked(low, 12 * ROWS), merge[...]
    )
    for i in range(3):
        for p in range(4):
            start = (4 * i + p) * ROWS
            out_div[i, p] = rows_s[start : start + NODES]

    @pl.when(has_below)
    def _():
        down_velocity.wait_send()
        down_stress.wait_send()

    @pl.when(has_above)
    def _():
        up_velocity.wait_send()
        up_share.wait_send()
        for k in range(3):
            tops[k].wait_send()

    for off in range(1, modes):
        share_copy(off).wait_send()
        whole_copy(off, mode).wait_send()


def on_device(doms, modes, velocity, stress, relax_time, viscosity, extensibility):
    ahead, back = column_tables()
    split, merge = order_tables()
    vmem = pl.BlockSpec(memory_space=pltpu.VMEM)
    smem = pl.BlockSpec(memory_space=pltpu.SMEM)
    dma = pltpu.SemaphoreType.DMA
    around_nodes = 2 * LANES
    scratch = [
        pltpu.VMEM((3, 3, NODES, around_nodes), BF16),
        pltpu.VMEM((3, 2, NODES, around_nodes), BF16),
        pltpu.VMEM((2, 6, NODES, around_nodes), BF16),
        pltpu.VMEM((12, 2 * 144 + WINDOW, LANES), BF16),
        pltpu.VMEM((3, 3 * 144 + WINDOW, LANES), BF16),
        pltpu.VMEM((9, 144 + WINDOW, LANES), BF16),
        pltpu.VMEM((4, POINTS, 6 * LANES), F32),
        pltpu.VMEM((4 * 256, 6 * LANES), BF16),
        pltpu.VMEM((3 * 256, 3 * LANES), BF16),
        pltpu.VMEM((4, 3, 256, 3 * LANES), BF16),
        pltpu.VMEM((4, 3, 9 * ROWS, 3 * LANES), F32),
        pltpu.VMEM((2, 3, POINTS, LANES), F32),
        pltpu.VMEM((2, 3, POINTS, LANES), BF16),
        pltpu.VMEM((2, 9, POINTS, LANES), F32),
        pltpu.VMEM((4, 9 * ROWS, 6 * LANES), F32),
        pltpu.VMEM((2, 9 * ROWS, 3 * LANES), F32),
        pltpu.VMEM((8, 3, ROWS, LANES), F32),
        pltpu.VMEM((8, 80, LANES), BF16),
        pltpu.VMEM((8, 80, LANES), BF16),
        pltpu.VMEM((8, 80, LANES), BF16),
        pltpu.VMEM((3, 2 * ROWS, LANES), BF16),
        pltpu.VMEM((3, 2 * ROWS, LANES), BF16),
        pltpu.VMEM((15, 2 * ROWS, LANES), BF16),
        pltpu.VMEM((15, 2 * ROWS, LANES), BF16),
        pltpu.VMEM((12 * ROWS, around_nodes), F32),
        dma((4,)),
        dma((4,)),
        dma((modes,)),
        dma((modes,)),
        dma((modes,)),
        dma((modes,)),
        dma((3,)),
        dma((3,)),
    ]
    return pl.pallas_call(
        functools.partial(kernel, doms, modes),
        out_shape=(
            jax.ShapeDtypeStruct(stress.shape, BF16),
            jax.ShapeDtypeStruct(velocity.shape, F32),
        ),
        in_specs=[vmem, vmem, smem, smem, smem, vmem, vmem, vmem, vmem, vmem],
        out_specs=(vmem, vmem),
        scratch_shapes=scratch,
        compiler_params=pltpu.CompilerParams(
            collective_id=0, has_side_effects=True, vmem_limit_bytes=48 * 1024 * 1024
        ),
        name="ptt",
    )(
        velocity,
        stress,
        relax_time,
        viscosity,
        extensibility,
        jnp.asarray(ahead),
        jnp.asarray(back),
        jnp.asarray(split),
        jnp.asarray(merge),
        jnp.asarray(inverse_mass()),
    )


def solution(mesh):
    return jax.shard_map(
        functools.partial(on_device, mesh.shape["dom"], mesh.shape["mode"]),
        mesh=mesh,
        in_specs=(P(None, "dom", None, None), P("mode", None, "dom", None, None), P(), P(), P()),
        out_specs=(P("mode", None, "dom", None, None), P(None, "dom", None, None)),
        check_vma=False,
    )
```

```python
import functools

import jax
import jax.numpy as jnp
import ml_dtypes
import numpy as np
from jax import lax
from jax.experimental import pallas as pl
from jax.experimental.pallas import tpu as pltpu
from jax.sharding import PartitionSpec as P

F32 = jnp.float32
BF16 = jnp.bfloat16
MESH = pl.DeviceIdType.MESH
SLOT = ((0, 3, 4), (3, 1, 5), (4, 5, 2))
NODES = 17
OWN = 4
GROUP = 72
SENT = 80
COLUMN = 216
WINDOW = 256
POINTS = 224
LANES = 128


def gauss_tables():
    s = np.array([0.5 - 0.5 * np.sqrt(0.6), 0.5, 0.5 + 0.5 * np.sqrt(0.6)])
    weight = np.array([5.0, 8.0, 5.0]) / 18.0
    value = np.stack([2.0 * s * s - 3.0 * s + 1.0, 4.0 * s * (1.0 - s), 2.0 * s * s - s], axis=1)
    slope = np.stack([4.0 * s - 3.0, 4.0 - 8.0 * s, 4.0 * s - 1.0], axis=1)

    def product(first, second, third):
        joined = (
            first[:, None, None, :, None, None]
            * second[None, :, None, None, :, None]
            * third[None, None, :, None, None, :]
        )
        return joined.reshape(27, 27)

    forward = np.concatenate(
        [
            product(value, value, value),
            product(slope, value, value),
            product(value, slope, value),
            product(value, value, slope),
        ],
        axis=0,
    )
    volume = (weight[:, None, None] * weight[None, :, None] * weight[None, None, :]).reshape(27)
    testing = (forward * np.tile(volume, 4)[:, None]).T
    return forward.astype(ml_dtypes.bfloat16), testing.astype(ml_dtypes.bfloat16)


def column_tables():
    forward, testing = (np.asarray(t, np.float32) for t in gauss_tables())
    ahead = np.zeros((2, 4, POINTS, WINDOW), np.float32)
    back = np.zeros((2, COLUMN, 4 * 256), np.float32)
    for layer, slots in enumerate(((0, 1, 2), (2, 3, 0))):
        for f in range((NODES - 1) // 2):
            for n in range(27):
                a, b, c = n // 9, (n // 3) % 3, n % 3
                node = GROUP * c + OWN * (2 * f + b) + slots[a]
                for d in range(4):
                    rows = slice(27 * d, 27 * d + 27)
                    ahead[layer, d, 27 * f : 27 * f + 27, node] = forward[rows, n]
                    back[layer, node, 256 * d + 27 * f : 256 * d + 27 * f + 27] = testing[n, rows]
    first = np.arange(WINDOW) % OWN == 0
    parts = np.zeros((2, POINTS, WINDOW), np.float32)
    parts[0] = ahead[1, 0] * ~first
    parts[1] = ahead[1, 0] * first
    ahead = np.concatenate([ahead.reshape(8, POINTS, WINDOW), parts])
    return ahead.astype(ml_dtypes.bfloat16), back.astype(ml_dtypes.bfloat16)


def order_tables():
    split = np.zeros((2 * LANES, 3 * LANES), np.float32)
    for g in range(LANES):
        split[2 * g, g] = 1.0
        split[2 * g + 1, LANES + g] = 1.0
        split[(2 * g + 2) % (2 * LANES), 2 * LANES + g] = 1.0
    merge = split[:, : 2 * LANES].T.copy()
    return split.astype(ml_dtypes.bfloat16), merge.astype(ml_dtypes.bfloat16)


def inverse_mass():
    r = np.arange(GROUP) // OWN
    mz = np.where(np.arange(GROUP) % 2 == 1, 2.0 / 3.0, 1.0 / 3.0)
    mr = np.where(r % 2 == 1, 2.0 / 3.0, np.where((r == 0) | (r >= NODES - 1), 1.0 / 6.0, 1.0 / 3.0))
    both = np.stack([3.0 / (mz * mr), 1.5 / (mz * mr)])
    return np.ascontiguousarray(np.broadcast_to(both[:, :, None], (2, GROUP, LANES))).astype(np.float32)


def dot(x, y):
    return jnp.dot(x, y, preferred_element_type=F32)


def raised(x, height):
    return jnp.concatenate([x, jnp.zeros((height - x.shape[0], x.shape[1]), F32)], axis=0).astype(BF16)


def column(c):
    return slice(LANES * c, LANES * (c + 1))


def kernel(
    doms,
    modes,
    velocity_hbm,
    stress_hbm,
    relax,
    viscosity,
    extension,
    ahead_hbm,
    back_hbm,
    split_hbm,
    mass_hbm,
    pieces,
    velocity,
    stress,
    ahead,
    back,
    split,
    inv_mass,
    s_rows,
    str_down,
    vel_above,
    vel_below,
    str_above,
    cup_send,
    cup_recv,
    top_send,
    top_recv,
    s_nodes,
    v_nodes,
    p_nodes,
    t_points,
    flux,
    dflux,
    derivs,
    grads,
    flow,
    winds,
    g_points,
    sums,
    devss,
    shares,
    rs_send,
    rs_recv,
    ag_buf,
    local_sem,
    halo_send,
    halo_recv,
    rs_ssem,
    rs_rsem,
    ag_ssem,
    ag_rsem,
    top_ssem,
    top_rsem,
):
    dom = lax.axis_index("dom")
    mode = lax.axis_index("mode")
    has_below = dom > 0
    has_above = dom < doms - 1
    below = (jnp.maximum(dom - 1, 0), mode)
    above = (jnp.minimum(dom + 1, doms - 1), mode)
    inside = jnp.where(has_below, 1.0, 0.0).astype(F32)

    barrier = pltpu.get_barrier_semaphore()

    @pl.when(has_below)
    def _():
        pl.semaphore_signal(barrier, inc=1, device_id=below, device_id_type=MESH)

    @pl.when(has_above)
    def _():
        pl.semaphore_signal(barrier, inc=1, device_id=above, device_id_type=MESH)

    for off in range(1, modes):
        peer = lax.rem(mode + off, modes)
        pl.semaphore_signal(barrier, inc=1, device_id=(dom, peer), device_id_type=MESH)

    pairs = (
        (velocity_hbm, velocity),
        (stress_hbm, stress),
        (split_hbm, split),
        (ahead_hbm, ahead),
        (back_hbm, back),
        (mass_hbm, inv_mass),
    )
    loads = [pltpu.make_async_copy(a, b, local_sem.at[k]) for k, (a, b) in enumerate(pairs)]
    for load in loads:
        load.start()

    def remote(src, dst, send, recv, target):
        return pltpu.make_async_remote_copy(
            src_ref=src,
            dst_ref=dst,
            send_sem=send,
            recv_sem=recv,
            device_id=target,
            device_id_type=MESH,
        )

    down_velocity = remote(velocity_hbm, vel_above, halo_send.at[0], halo_recv.at[0], below)
    down_stress = remote(str_down, str_above, halo_send.at[1], halo_recv.at[1], below)
    up_velocity = remote(velocity_hbm, vel_below, halo_send.at[2], halo_recv.at[2], above)
    up_share = remote(cup_send, cup_recv, halo_send.at[3], halo_recv.at[3], above)

    @pl.when(jnp.logical_not(has_above))
    def _():
        vel_above[...] = jnp.zeros_like(vel_above)
        str_above[...] = jnp.zeros_like(str_above)

    @pl.when(jnp.logical_not(has_below))
    def _():
        vel_below[...] = jnp.zeros_like(vel_below)
        cup_recv[...] = jnp.zeros_like(cup_recv)
        top_recv[...] = jnp.zeros_like(top_recv)

    slot = lax.rem(lax.broadcasted_iota(jnp.int32, (GROUP, LANES), 0), OWN)
    slots = jnp.concatenate([slot, slot], axis=1)
    first = slot == 0
    firsts = slots == 0

    def shifted(block, rows):
        return block if rows == 0 else pltpu.roll(block, rows % GROUP, axis=0)

    def packed(blocks):
        result = blocks[0]
        for q in range(1, len(blocks)):
            result = jnp.where(slots == q, shifted(blocks[q], q), result)
        return result

    def rows_of(ref):
        return jnp.concatenate(
            [ref.astype(F32).reshape(OWN * NODES, 2 * LANES), jnp.zeros((GROUP - OWN * NODES, 2 * LANES), F32)],
            axis=0,
        )

    loads[1].wait()
    for g in range(3):
        blocks = []
        for q in range(4):
            k = 4 * g + q
            blocks.append(rows_of(stress[k // 6, k % 6]))
            s_rows[k] = raised(blocks[q], SENT)
        str_down[g] = raised(packed(blocks), SENT)

    def laid_out(rows):
        spread = dot(jnp.concatenate(rows, axis=0), split[...])
        return [
            [spread[SENT * k : SENT * k + GROUP, column(c)] for c in range(3)] for k in range(len(rows))
        ]

    def window(parts):
        return raised(jnp.concatenate(parts, axis=0), WINDOW)

    for d in range(4):
        flux[256 * d + POINTS : 256 * (d + 1)] = jnp.zeros((256 - POINTS, 6 * LANES), BF16)
        derivs[d, POINTS:] = jnp.zeros((256 - POINTS, 9 * LANES), BF16)
    for d in range(3):
        dflux[256 * d + POINTS : 256 * (d + 1)] = jnp.zeros((256 - POINTS, 3 * LANES), BF16)

    loads[2].wait()
    for k in range(4):
        own = laid_out([s_rows[3 * k + c] for c in range(3)])
        for c in range(3):
            s_nodes[0, 3 * k + c] = window(own[c])

    def side(ref, index, count):
        return jnp.concatenate([ref[index, c] for c in range(count)], axis=1)

    def stress_window(layer, m):
        return jnp.concatenate([s_nodes[layer, 6 * m + c] for c in range(6)], axis=1)

    def around(result, c):
        even = result[0:GROUP, column(c)] + pltpu.roll(result[2 * GROUP :, column(c)], 1, axis=1)
        return even, result[GROUP : 2 * GROUP, column(c)]

    def points_of(layer):
        for m in range(2):
            nodes = stress_window(layer, m)
            for d in range(4):
                t_points[layer, m, d] = dot(ahead[4 * layer + d], nodes)

    def into_dflux(values):
        for j in range(3):
            for i in range(3):
                dflux[256 * j : 256 * j + POINTS, column(i)] = values[SLOT[i][j]]

    loads[0].wait()
    own_velocity = laid_out([raised(rows_of(velocity[i]), SENT) for i in range(3)])
    for i in range(3):
        v_nodes[0, i] = window(own_velocity[i])

    others = modes - 1 + has_below.astype(jnp.int32) + has_above.astype(jnp.int32)
    pl.semaphore_wait(barrier, others)

    @pl.when(has_below)
    def _():
        down_velocity.start()
        down_stress.start()

    @pl.when(has_above)
    def _():
        up_velocity.start()

    loads[3].wait()
    loads[4].wait()
    both = jnp.concatenate([stress_window(0, 0), stress_window(0, 1)], axis=0)

    def outer_share(part):
        at = dot(jnp.concatenate([part, part], axis=1), both).astype(BF16)
        into_dflux([at[:, column(c)] for c in range(6)])
        return dot(back[1, :, 256:], dflux[...])

    outer = outer_share(ahead[8])
    cup_send[...] = raised(packed([jnp.concatenate(around(outer, i), axis=1) for i in range(3)]), SENT)

    @pl.when(has_above)
    def _():
        up_share.start()

    outer = outer_share(ahead[9])
    for i in range(3):
        even, odd = around(outer, i)
        zero = jnp.zeros_like(even)
        shares[GROUP * 2 * i : GROUP * (2 * i + 1)] = jnp.where(first, even * inside, zero)
        shares[GROUP * (2 * i + 1) : GROUP * (2 * i + 2)] = jnp.where(first, odd * inside, zero)

    def add_shares(result):
        for i in range(3):
            even, odd = around(result, i)
            shares[GROUP * 2 * i : GROUP * (2 * i + 1)] += even
            shares[GROUP * (2 * i + 1) : GROUP * (2 * i + 2)] += odd

    at = dot(jnp.concatenate([ahead[0], ahead[0]], axis=1), both).astype(BF16)
    into_dflux([at[:, column(c)] for c in range(6)])
    add_shares(dot(back[0, :, 256:], dflux[...]))

    def velocity_points(layer, at):
        at = at.astype(BF16).astype(F32)
        u = [at[:, column(i)] for i in range(3)]
        upwind = 0.5 / (1.0 + jnp.sqrt(u[0] * u[0] + u[1] * u[1] + u[2] * u[2]))
        for i in range(3):
            flow[layer, i] = u[i]
            winds[layer, i] = (upwind * u[i]).astype(BF16)

    def gradient_points(variant, layer):
        nodes = side(v_nodes, variant, 3)
        for j in range(3):
            at = dot(ahead[4 * layer + 1 + j], nodes)
            derivs[variant, 0:POINTS, 3 * LANES * j : 3 * LANES * (j + 1)] = at.astype(BF16)
        grads[variant] = dot(back[layer, :, 0:256], derivs[variant])

    velocity_points(0, dot(ahead[0], side(v_nodes, 0, 3)))
    gradient_points(0, 0)
    points_of(0)

    @pl.when(has_above)
    def _():
        down_velocity.wait_recv()

    @pl.when(has_below)
    def _():
        up_velocity.wait_recv()

    six = laid_out([raised(rows_of(ref[i]), SENT) for ref in (vel_above, vel_below) for i in range(3)])
    higher, lower = six[0:3], six[3:6]
    own = [
        [v_nodes[0, i, 0:224].astype(F32)[GROUP * c : GROUP * (c + 1)] for c in range(3)]
        for i in range(3)
    ]
    for i in range(3):
        v_nodes[1, i] = window([jnp.where(first, higher[i][c], own[i][c]) for c in range(3)])
        v_nodes[2, i] = window([jnp.where(first, own[i][c], lower[i][c]) for c in range(3)])
        v_nodes[3, i] = window(higher[i])
    gradient_points(1, 1)
    gradient_points(2, 1)
    gradient_points(3, 0)

    @pl.when(has_above)
    def _():
        down_stress.wait_recv()

    higher = laid_out([str_above[g] for g in range(3)])
    for k in range(12):
        mine = s_nodes[0, k].astype(F32)
        s_nodes[1, k] = window(
            [
                jnp.where(
                    first, shifted(higher[k // 4][c], -(k % 4)), mine[GROUP * c : GROUP * (c + 1)]
                )
                for c in range(3)
            ]
        )
    both = jnp.concatenate([stress_window(1, 0), stress_window(1, 1)], axis=0)
    at = dot(jnp.concatenate([ahead[4], ahead[4]], axis=1), both).astype(BF16)
    into_dflux([at[:, column(c)] for c in range(6)])
    upper = dot(back[1, :, 256:], dflux[...])

    @pl.when(has_below)
    def _():
        up_share.wait_recv()

    from_below = cup_recv[...].astype(F32)[0:GROUP]
    for i in range(3):
        even, odd = around(upper, i)
        arrived = shifted(from_below, -i)
        shares[GROUP * 2 * i : GROUP * (2 * i + 1)] += jnp.where(first, arrived[:, 0:LANES], even)
        shares[GROUP * (2 * i + 1) : GROUP * (2 * i + 2)] += jnp.where(first, arrived[:, LANES:], odd)
    for k in range(8):
        rs_send[k] = raised(shares[56 * k : 56 * (k + 1)], 64)

    def share_copy(off):
        peer = lax.rem(mode + off, modes)
        return remote(
            rs_send.at[peer], rs_recv.at[off], rs_ssem.at[off], rs_rsem.at[off], (dom, peer)
        )

    for off in range(1, modes):
        share_copy(off).start()

    loads[5].wait()
    start_mass = jnp.where(first, jnp.where(has_below, 1.0, 2.0).astype(F32), jnp.ones((GROUP, LANES), F32))
    end_mass = jnp.where(has_above, 1.0, 0.0).astype(F32)

    def project(j, _):
        for i in range(3):
            cols = pl.ds(pl.multiple_of((3 * j + i) * LANES, LANES), LANES)
            mine, over = [], []
            for c in range(3):
                rows = slice(GROUP * c, GROUP * (c + 1))
                upper = grads[1, rows, cols]
                mine.append(grads[0, rows, cols] + jnp.where(first, grads[2, rows, cols] * inside, upper))
                over.append(grads[3, rows, cols] + upper)
            results = []
            for parts, scale in ((mine, start_mass), (over, end_mass)):
                even = (parts[0] + pltpu.roll(parts[2], 1, axis=1)) * (inv_mass[0] * scale)
                odd = parts[1] * (inv_mass[1] * scale)
                results.append([even, odd, pltpu.roll(even, LANES - 1, axis=1)])
            p_nodes[0, 3 * i + j] = window(results[0])
            p_nodes[1, 3 * i + j] = window(
                [jnp.where(first, results[1][c], results[0][c]) for c in range(3)]
            )
        return 0

    lax.fori_loop(0, 3, project, 0)

    def projected_points(layer):
        for i in range(3):
            nodes = jnp.concatenate([p_nodes[layer, 3 * i + j] for j in range(3)], axis=1)
            here = dot(ahead[4 * layer], nodes)
            for j in range(3):
                g_points[layer, 3 * i + j] = here[:, column(j)]

    projected_points(1)
    velocity_points(1, dot(ahead[4], side(v_nodes, 1, 3)))

    def residual_of(layer, m):
        lam = jnp.full((16, LANES), relax[2 * mode + m], F32)
        eta = jnp.full((16, LANES), viscosity[2 * mode + m], F32)
        eps = jnp.full((16, LANES), extension[2 * mode + m], F32)
        half = 0.5 / lam
        slope = 0.5 * eps / eta
        kappa = eta / lam

        def chunk(start):
            rows = pl.ds(start, 16)
            t = [t_points[layer, m, 0, rows, column(c)] for c in range(6)]
            g = [[g_points[layer, 3 * i + j, rows] for j in range(3)] for i in range(3)]
            u = [flow[layer, i, rows] for i in range(3)]
            y = half + slope * (t[0] + t[1] + t[2])
            shift = (y * kappa) * 2.0
            tt = [t[0] + kappa, t[1] + kappa, t[2] + kappa] + t[3:]
            h = [g[k][k] - y for k in range(3)]

            def entry(i, j):
                return tt[SLOT[i][j]]

            for c, (i, j) in enumerate(((0, 0), (1, 1), (2, 2), (0, 1), (0, 2), (1, 2))):
                value = u[0] * t_points[layer, m, 1, rows, column(c)]
                value = value + u[1] * t_points[layer, m, 2, rows, column(c)]
                value = value + u[2] * t_points[layer, m, 3, rows, column(c)]
                if i == j:
                    k, l = (i + 1) % 3, (i + 2) % 3
                    part = h[i] * entry(i, i) + g[i][k] * entry(k, i) + g[i][l] * entry(l, i)
                    value = value - (part + part) - shift
                else:
                    k = 3 - i - j
                    part = (h[i] + h[j]) * entry(i, j)
                    part = part + g[i][j] * entry(j, j) + g[i][k] * entry(k, j)
                    part = part + g[j][i] * entry(i, i) + g[j][k] * entry(k, i)
                    value = value - part
                rounded = value.astype(BF16)
                flux[rows, column(c)] = rounded
                for j2 in range(3):
                    place = pl.ds(256 * (1 + j2) + start, 16)
                    flux[place, column(c)] = rounded * winds[layer, j2, rows]

        def step(k, _):
            chunk(pl.multiple_of(16 * k, 16))
            return 0

        lax.fori_loop(0, POINTS // 16, step, 0, unroll=True)
        sums[layer, m] = dot(back[layer], flux[...])

    weight = viscosity[0]
    for k in range(1, 2 * modes):
        weight = weight + viscosity[k]
    weight = weight * (1.0 / (2 * modes))

    def devss_of(layer):
        values = [None] * 6
        for i in range(3):
            for j in range(i, 3):
                d_ij = derivs[layer, 0:POINTS, column(3 * j + i)].astype(F32)
                d_ji = derivs[layer, 0:POINTS, column(3 * i + j)].astype(F32)
                excess = d_ij + d_ji - g_points[layer, 3 * i + j] - g_points[layer, 3 * j + i]
                values[SLOT[i][j]] = (weight * excess).astype(BF16)
        into_dflux(values)
        devss[layer] = dot(back[layer, :, 256:], dflux[...])

    tops = [
        remote(top_send.at[k], top_recv.at[k], top_ssem.at[k], top_rsem.at[k], above) for k in range(4)
    ]

    points_of(1)
    devss_of(1)
    for m in range(2):
        residual_of(1, m)
        result = sums[1, m]
        blocks = [jnp.concatenate(around(result, c), axis=1) for c in range(6)]
        result = devss[1]
        for i in ((0, 1), (2,))[m]:
            blocks.append(jnp.concatenate(around(result, i), axis=1))
        top_send[2 * m] = raised(packed(blocks[0:4]), SENT)
        top_send[2 * m + 1] = raised(packed(blocks[4:]), SENT)

        @pl.when(has_above)
        def _():
            tops[2 * m].start()
            tops[2 * m + 1].start()

    def sum_shares():
        place = pl.ds(pl.multiple_of(mode * 56, 8), 56)
        total = jnp.concatenate([shares[place], jnp.zeros((8, LANES), F32)], axis=0)
        for off in range(1, modes):
            share_copy(off).wait_recv()
            total = total + rs_recv[off].astype(F32)
        ag_buf[mode] = total.astype(BF16)

    def whole_copy(off, place):
        peer = lax.rem(mode + off, modes)
        return remote(
            ag_buf.at[place], ag_buf.at[place], ag_ssem.at[off], ag_rsem.at[off], (dom, peer)
        )

    sum_shares()
    for off in range(1, modes):
        whole_copy(off, mode).start()

    projected_points(0)
    devss_of(0)
    for m in range(2):
        residual_of(0, m)

    for off in range(1, modes):
        whole_copy(off, lax.rem(mode + modes - off, modes)).wait_recv()

    @pl.when(has_below)
    def _():
        for k in range(4):
            tops[k].wait_recv()

    def nodes_of(lower, upper, c, arrived):
        low = jnp.concatenate(around(lower, c), axis=1)
        high = jnp.concatenate(around(upper, c), axis=1)
        return low + jnp.where(firsts, arrived, high)

    def finish(m, _):
        lam = relax[2 * mode + m]
        lower, upper = sums[0, m], sums[1, m]
        arrived = [top_recv[2 * m + k].astype(F32)[0:GROUP] for k in range(2)]
        for c in range(6):
            both = nodes_of(lower, upper, c, shifted(arrived[c // 4], -(c % 4)))
            pieces[6 * m + c] = raised(both * lam, SENT)
        return 0

    lax.fori_loop(0, 2, finish, 0)

    for k in range(8):
        shares[56 * k : 56 * (k + 1)] = ag_buf[k].astype(F32)[0:56]
    lower, upper = devss[0], devss[1]
    for i in range(3):
        group, place = ((1, 2), (1, 3), (3, 2))[i]
        arrived = shifted(top_recv[group].astype(F32)[0:GROUP], -place)
        both = nodes_of(lower, upper, i, arrived)
        both = both + jnp.concatenate(
            [
                shares[GROUP * 2 * i : GROUP * (2 * i + 1)],
                shares[GROUP * (2 * i + 1) : GROUP * (2 * i + 2)],
            ],
            axis=1,
        )
        rounded = both.astype(BF16).astype(F32)
        pieces[12 + i] = raised(rounded, SENT)
        pieces[15 + i] = raised(both - rounded, SENT)

    @pl.when(has_below)
    def _():
        down_velocity.wait_send()
        down_stress.wait_send()

    @pl.when(has_above)
    def _():
        up_velocity.wait_send()
        up_share.wait_send()
        for k in range(4):
            tops[k].wait_send()

    for off in range(1, modes):
        share_copy(off).wait_send()
        whole_copy(off, mode).wait_send()


def finish_kernel(pieces, merge, out_stress, out_div):
    def merged(k):
        rows = dot(pieces[k], merge[...])[0 : OWN * NODES]
        return rows.reshape(NODES, OWN, 2 * LANES)

    for k in range(12):
        out_stress[k // 6, k % 6] = merged(k).astype(BF16)
    for i in range(3):
        out_div[i] = merged(12 + i) + merged(15 + i)


def on_device(doms, modes, velocity, stress, relax_time, viscosity, extensibility):
    ahead, back = column_tables()
    split, merge = order_tables()
    velocity = jnp.transpose(velocity, (0, 2, 1, 3))
    stress = jnp.transpose(stress, (0, 1, 3, 2, 4))
    vmem = pl.BlockSpec(memory_space=pltpu.VMEM)
    smem = pl.BlockSpec(memory_space=pltpu.SMEM)
    hbm = pl.BlockSpec(memory_space=pltpu.HBM)
    dma = pltpu.SemaphoreType.DMA
    around_nodes = 2 * LANES
    scratch = [
        pltpu.VMEM(velocity.shape, BF16),
        pltpu.VMEM(stress.shape, BF16),
        pltpu.VMEM(ahead.shape, BF16),
        pltpu.VMEM(back.shape, BF16),
        pltpu.VMEM(split.shape, BF16),
        pltpu.VMEM((2, GROUP, LANES), F32),
        pltpu.VMEM((12, SENT, around_nodes), BF16),
        pltpu.VMEM((3, SENT, around_nodes), BF16),
        pltpu.VMEM(velocity.shape, BF16),
        pltpu.VMEM(velocity.shape, BF16),
        pltpu.VMEM((3, SENT, around_nodes), BF16),
        pltpu.VMEM((SENT, around_nodes), BF16),
        pltpu.VMEM((SENT, around_nodes), BF16),
        pltpu.VMEM((4, SENT, around_nodes), BF16),
        pltpu.VMEM((4, SENT, around_nodes), BF16),
        pltpu.VMEM((2, 12, WINDOW, LANES), BF16),
        pltpu.VMEM((4, 3, WINDOW, LANES), BF16),
        pltpu.VMEM((2, 9, WINDOW, LANES), BF16),
        pltpu.VMEM((2, 2, 4, POINTS, 6 * LANES), F32),
        pltpu.VMEM((4 * 256, 6 * LANES), BF16),
        pltpu.VMEM((3 * 256, 3 * LANES), BF16),
        pltpu.VMEM((4, 256, 9 * LANES), BF16),
        pltpu.VMEM((4, COLUMN, 9 * LANES), F32),
        pltpu.VMEM((2, 3, POINTS, LANES), F32),
        pltpu.VMEM((2, 3, POINTS, LANES), BF16),
        pltpu.VMEM((2, 9, POINTS, LANES), F32),
        pltpu.VMEM((2, 2, COLUMN, 6 * LANES), F32),
        pltpu.VMEM((2, COLUMN, 3 * LANES), F32),
        pltpu.VMEM((448, LANES), F32),
        pltpu.VMEM((8, 64, LANES), BF16),
        pltpu.VMEM((8, 64, LANES), BF16),
        pltpu.VMEM((8, 64, LANES), BF16),
        dma((6,)),
        dma((4,)),
        dma((4,)),
        dma((modes,)),
        dma((modes,)),
        dma((modes,)),
        dma((modes,)),
        dma((4,)),
        dma((4,)),
    ]
    pieces = pl.pallas_call(
        functools.partial(kernel, doms, modes),
        out_shape=pltpu.VMEM((18, SENT, around_nodes), BF16),
        in_specs=[hbm, hbm, smem, smem, smem, hbm, hbm, hbm, hbm],
        out_specs=vmem,
        scratch_shapes=scratch,
        compiler_params=pltpu.CompilerParams(
            collective_id=0, has_side_effects=True, vmem_limit_bytes=58 * 1024 * 1024
        ),
        name="ptt",
    )(
        velocity,
        stress,
        relax_time,
        viscosity,
        extensibility,
        jnp.asarray(ahead),
        jnp.asarray(back),
        jnp.asarray(split),
        jnp.asarray(inverse_mass()),
    )
    out_stress, out_div = pl.pallas_call(
        finish_kernel,
        out_shape=(
            jax.ShapeDtypeStruct(stress.shape, BF16),
            jax.ShapeDtypeStruct(velocity.shape, F32),
        ),
        in_specs=[vmem, vmem],
        out_specs=(vmem, vmem),
        compiler_params=pltpu.CompilerParams(vmem_limit_bytes=16 * 1024 * 1024),
        name="finish",
    )(pieces, jnp.asarray(merge))
    return jnp.transpose(out_stress, (0, 1, 3, 2, 4)), jnp.transpose(out_div, (0, 2, 1, 3))


def solution(mesh):
    return jax.shard_map(
        functools.partial(on_device, mesh.shape["dom"], mesh.shape["mode"]),
        mesh=mesh,
        in_specs=(P(None, "dom", None, None), P("mode", None, "dom", None, None), P(), P(), P()),
        out_specs=(P("mode", None, "dom", None, None), P(None, "dom", None, None)),
        check_vma=False,
    )
```

```python
import functools

import jax
import jax.numpy as jnp
import ml_dtypes
import numpy as np
from jax import lax
from jax.experimental import pallas as pl
from jax.experimental.pallas import tpu as pltpu
from jax.sharding import PartitionSpec as P

F32 = jnp.float32
BF16 = jnp.bfloat16
MESH = pl.DeviceIdType.MESH
SLOT = ((0, 3, 4), (3, 1, 5), (4, 5, 2))
NODES = 17
OWN = 4
GROUP = 72
SENT = 80
COLUMN = 216
WINDOW = 256
POINTS = 224
LANES = 128


def gauss_tables():
    s = np.array([0.5 - 0.5 * np.sqrt(0.6), 0.5, 0.5 + 0.5 * np.sqrt(0.6)])
    weight = np.array([5.0, 8.0, 5.0]) / 18.0
    value = np.stack([2.0 * s * s - 3.0 * s + 1.0, 4.0 * s * (1.0 - s), 2.0 * s * s - s], axis=1)
    slope = np.stack([4.0 * s - 3.0, 4.0 - 8.0 * s, 4.0 * s - 1.0], axis=1)

    def product(first, second, third):
        joined = (
            first[:, None, None, :, None, None]
            * second[None, :, None, None, :, None]
            * third[None, None, :, None, None, :]
        )
        return joined.reshape(27, 27)

    forward = np.concatenate(
        [
            product(value, value, value),
            product(slope, value, value),
            product(value, slope, value),
            product(value, value, slope),
        ],
        axis=0,
    )
    volume = (weight[:, None, None] * weight[None, :, None] * weight[None, None, :]).reshape(27)
    testing = (forward * np.tile(volume, 4)[:, None]).T
    return forward.astype(ml_dtypes.bfloat16), testing.astype(ml_dtypes.bfloat16)


def column_tables():
    forward, testing = (np.asarray(t, np.float32) for t in gauss_tables())
    ahead = np.zeros((2, 4, POINTS, WINDOW), np.float32)
    back = np.zeros((2, COLUMN, 4 * 256), np.float32)
    for layer, slots in enumerate(((0, 1, 2), (2, 3, 0))):
        for f in range((NODES - 1) // 2):
            for n in range(27):
                a, b, c = n // 9, (n // 3) % 3, n % 3
                node = GROUP * c + OWN * (2 * f + b) + slots[a]
                for d in range(4):
                    rows = slice(27 * d, 27 * d + 27)
                    ahead[layer, d, 27 * f : 27 * f + 27, node] = forward[rows, n]
                    back[layer, node, 256 * d + 27 * f : 256 * d + 27 * f + 27] = testing[n, rows]
    first = np.arange(WINDOW) % OWN == 0
    parts = np.zeros((2, POINTS, WINDOW), np.float32)
    parts[0] = ahead[1, 0] * ~first
    parts[1] = ahead[1, 0] * first
    ahead = np.concatenate([ahead.reshape(8, POINTS, WINDOW), parts])
    return ahead.astype(ml_dtypes.bfloat16), back.astype(ml_dtypes.bfloat16)


def order_tables():
    split = np.zeros((2 * LANES, 3 * LANES), np.float32)
    for g in range(LANES):
        split[2 * g, g] = 1.0
        split[2 * g + 1, LANES + g] = 1.0
        split[(2 * g + 2) % (2 * LANES), 2 * LANES + g] = 1.0
    merge = split[:, : 2 * LANES].T.copy()
    return split.astype(ml_dtypes.bfloat16), merge.astype(ml_dtypes.bfloat16)


def inverse_mass():
    r = np.arange(GROUP) // OWN
    mz = np.where(np.arange(GROUP) % 2 == 1, 2.0 / 3.0, 1.0 / 3.0)
    mr = np.where(r % 2 == 1, 2.0 / 3.0, np.where((r == 0) | (r >= NODES - 1), 1.0 / 6.0, 1.0 / 3.0))
    both = np.stack([3.0 / (mz * mr), 1.5 / (mz * mr)])
    return np.ascontiguousarray(np.broadcast_to(both[:, :, None], (2, GROUP, LANES))).astype(np.float32)


def dot(x, y):
    return jnp.dot(x, y, preferred_element_type=F32)


def raised(x, height):
    return jnp.concatenate([x, jnp.zeros((height - x.shape[0], x.shape[1]), F32)], axis=0).astype(BF16)


def column(c):
    return slice(LANES * c, LANES * (c + 1))


def kernel(
    doms,
    modes,
    velocity_hbm,
    stress_hbm,
    relax,
    viscosity,
    extension,
    ahead_hbm,
    back_hbm,
    split_hbm,
    mass_hbm,
    pieces,
    velocity,
    stress,
    ahead,
    back,
    split,
    inv_mass,
    s_rows,
    str_down,
    vel_above,
    vel_below,
    str_above,
    cup_send,
    cup_recv,
    top_send,
    top_recv,
    s_nodes,
    v_nodes,
    p_nodes,
    t_points,
    flux,
    dflux,
    masked,
    derivs,
    grads,
    flow,
    winds,
    g_points,
    sums,
    devss,
    shares,
    rs_send,
    rs_recv,
    ag_buf,
    local_sem,
    halo_send,
    halo_recv,
    rs_ssem,
    rs_rsem,
    ag_ssem,
    ag_rsem,
    top_ssem,
    top_rsem,
):
    dom = lax.axis_index("dom")
    mode = lax.axis_index("mode")
    has_below = dom > 0
    has_above = dom < doms - 1
    below = (jnp.maximum(dom - 1, 0), mode)
    above = (jnp.minimum(dom + 1, doms - 1), mode)
    inside = jnp.where(has_below, 1.0, 0.0).astype(F32)

    barrier = pltpu.get_barrier_semaphore()

    @pl.when(has_below)
    def _():
        pl.semaphore_signal(barrier, inc=1, device_id=below, device_id_type=MESH)

    @pl.when(has_above)
    def _():
        pl.semaphore_signal(barrier, inc=1, device_id=above, device_id_type=MESH)

    for off in range(1, modes):
        peer = lax.rem(mode + off, modes)
        pl.semaphore_signal(barrier, inc=1, device_id=(dom, peer), device_id_type=MESH)

    pairs = (
        (stress_hbm.at[0], stress.at[0]),
        (stress_hbm.at[1], stress.at[1]),
        (split_hbm, split),
        (ahead_hbm.at[pl.ds(8, 2)], ahead.at[pl.ds(8, 2)]),
        (ahead_hbm.at[pl.ds(0, 4)], ahead.at[pl.ds(0, 4)]),
        (back_hbm.at[1], back.at[1]),
        (back_hbm.at[0], back.at[0]),
        (velocity_hbm, velocity),
        (ahead_hbm.at[pl.ds(4, 4)], ahead.at[pl.ds(4, 4)]),
        (mass_hbm, inv_mass),
    )
    loads = [pltpu.make_async_copy(a, b, local_sem.at[k]) for k, (a, b) in enumerate(pairs)]

    def arrived_here(*which):
        for k in which:
            loads[k].wait()

    for load in loads:
        load.start()

    def remote(src, dst, send, recv, target):
        return pltpu.make_async_remote_copy(
            src_ref=src,
            dst_ref=dst,
            send_sem=send,
            recv_sem=recv,
            device_id=target,
            device_id_type=MESH,
        )

    down_velocity = remote(velocity_hbm, vel_above, halo_send.at[0], halo_recv.at[0], below)
    down_stress = remote(str_down, str_above, halo_send.at[1], halo_recv.at[1], below)
    up_velocity = remote(velocity_hbm, vel_below, halo_send.at[2], halo_recv.at[2], above)
    up_share = remote(cup_send, cup_recv, halo_send.at[3], halo_recv.at[3], above)

    @pl.when(jnp.logical_not(has_above))
    def _():
        vel_above[...] = jnp.zeros_like(vel_above)
        str_above[...] = jnp.zeros_like(str_above)

    @pl.when(jnp.logical_not(has_below))
    def _():
        vel_below[...] = jnp.zeros_like(vel_below)
        cup_recv[...] = jnp.zeros_like(cup_recv)
        top_recv[...] = jnp.zeros_like(top_recv)

    slot = lax.rem(lax.broadcasted_iota(jnp.int32, (GROUP, LANES), 0), OWN)
    slots = jnp.concatenate([slot, slot], axis=1)
    first = slot == 0
    firsts = slots == 0

    def shifted(block, rows):
        return block if rows == 0 else pltpu.roll(block, rows % GROUP, axis=0)

    def packed(blocks):
        result = blocks[0]
        for q in range(1, len(blocks)):
            result = jnp.where(slots == q, shifted(blocks[q], q), result)
        return result

    def rows_of(ref):
        return jnp.concatenate(
            [ref.astype(F32).reshape(OWN * NODES, 2 * LANES), jnp.zeros((GROUP - OWN * NODES, 2 * LANES), F32)],
            axis=0,
        )

    arrived_here(0, 1)
    for g in range(3):
        blocks = []
        for q in range(4):
            k = 4 * g + q
            blocks.append(rows_of(stress[k // 6, k % 6]))
            s_rows[k] = raised(blocks[q], SENT)
        str_down[g] = raised(packed(blocks), SENT)

    def laid_out(rows):
        spread = dot(jnp.concatenate(rows, axis=0), split[...])
        return [
            [spread[SENT * k : SENT * k + GROUP, column(c)] for c in range(3)] for k in range(len(rows))
        ]

    def window(parts):
        return raised(jnp.concatenate(parts, axis=0), WINDOW)

    for d in range(4):
        flux[256 * d + POINTS : 256 * (d + 1)] = jnp.zeros((256 - POINTS, 6 * LANES), BF16)
        derivs[d, POINTS:] = jnp.zeros((256 - POINTS, 9 * LANES), BF16)
    for d in range(9):
        dflux[256 * d + POINTS : 256 * (d + 1)] = jnp.zeros((256 - POINTS, 3 * LANES), BF16)

    arrived_here(2)
    for k in range(4):
        own = laid_out([s_rows[3 * k + c] for c in range(3)])
        for c in range(3):
            s_nodes[0, 3 * k + c] = window(own[c])

    def side(ref, index, count):
        return jnp.concatenate([ref[index, c] for c in range(count)], axis=1)

    def stress_window(layer, m):
        return jnp.concatenate([s_nodes[layer, 6 * m + c] for c in range(6)], axis=1)

    def around(result, c):
        even = result[0:GROUP, column(c)] + pltpu.roll(result[2 * GROUP :, column(c)], 1, axis=1)
        return even, result[GROUP : 2 * GROUP, column(c)]

    def points_of(layer, m, d):
        t_points[layer, m, d] = dot(ahead[4 * layer + d], stress_window(layer, m))

    def into(ref, values):
        for j in range(3):
            for i in range(3):
                ref[256 * j : 256 * j + POINTS, column(i)] = values[SLOT[i][j]]

    others = modes - 1 + has_below.astype(jnp.int32) + has_above.astype(jnp.int32)
    pl.semaphore_wait(barrier, others)

    @pl.when(has_below)
    def _():
        down_velocity.start()

    @pl.when(has_above)
    def _():
        up_velocity.start()

    @pl.when(has_below)
    def _():
        down_stress.start()

    arrived_here(3, 4, 5, 6)
    both = jnp.concatenate([stress_window(0, 0), stress_window(0, 1)], axis=0)
    parts = jnp.concatenate([ahead[8], ahead[9], ahead[0]], axis=0)
    at = dot(jnp.concatenate([parts, parts], axis=1), both)
    for part in range(3):
        here = at[POINTS * part : POINTS * (part + 1)]
        if part == 1:
            here = here * inside
        here = here.astype(BF16)
        into(dflux.at[pl.ds(768 * part, 768)], [here[:, column(c)] for c in range(6)])
    outer = dot(back[1, :, 256:], dflux[0:768])
    for k in range(3):
        rows = slice(GROUP * k, GROUP * (k + 1))
        own = back[1, rows].astype(F32)
        zero = jnp.zeros_like(own)
        is_first = jnp.concatenate([first] * 8, axis=1)
        masked[0, rows] = jnp.where(is_first, own, zero)
        masked[1, rows] = jnp.where(is_first, zero, own[:, 0:1024])
    tested = jnp.concatenate([masked[0, :, 256:].astype(BF16), back[0, :, 256:]], axis=1)
    local = dot(tested, dflux[768:])
    cup_send[...] = raised(packed([jnp.concatenate(around(outer, i), axis=1) for i in range(3)]), SENT)

    @pl.when(has_above)
    def _():
        up_share.start()

    for i in range(3):
        even, odd = around(local, i)
        shares[GROUP * 2 * i : GROUP * (2 * i + 1)] = even
        shares[GROUP * (2 * i + 1) : GROUP * (2 * i + 2)] = odd

    def velocity_points(layer, at):
        at = at.astype(BF16).astype(F32)
        u = [at[:, column(i)] for i in range(3)]
        upwind = 0.5 / (1.0 + jnp.sqrt(u[0] * u[0] + u[1] * u[1] + u[2] * u[2]))
        for i in range(3):
            flow[layer, i] = u[i]
            winds[layer, i] = (upwind * u[i]).astype(BF16)

    def gradient_points(variant, layer):
        nodes = side(v_nodes, variant, 3)
        for j in range(3):
            at = dot(ahead[4 * layer + 1 + j], nodes)
            derivs[variant, 0:POINTS, 3 * LANES * j : 3 * LANES * (j + 1)] = at.astype(BF16)

    arrived_here(7)
    own_velocity = laid_out([raised(rows_of(velocity[i]), SENT) for i in range(3)])
    for i in range(3):
        v_nodes[0, i] = window(own_velocity[i])

    velocity_points(0, dot(ahead[0], side(v_nodes, 0, 3)))
    gradient_points(0, 0)

    @pl.when(has_above)
    def _():
        down_velocity.wait_recv()

    @pl.when(has_below)
    def _():
        up_velocity.wait_recv()

    six = laid_out([raised(rows_of(ref[i]), SENT) for ref in (vel_above, vel_below) for i in range(3)])
    higher, lower = six[0:3], six[3:6]
    own = [
        [v_nodes[0, i, 0:224].astype(F32)[GROUP * c : GROUP * (c + 1)] for c in range(3)]
        for i in range(3)
    ]
    for i in range(3):
        v_nodes[1, i] = window([jnp.where(first, higher[i][c], own[i][c]) for c in range(3)])
        v_nodes[2, i] = window([jnp.where(first, own[i][c] * inside, lower[i][c]) for c in range(3)])
        v_nodes[3, i] = window(higher[i])
    arrived_here(8)
    gradient_points(1, 1)
    gradient_points(2, 1)
    gradient_points(3, 0)
    tested = jnp.concatenate(
        [back[0, :, 0:256], masked[1, :, 0:256].astype(BF16), masked[0, :, 0:256].astype(BF16)], axis=1
    )
    grads[0] = dot(tested, jnp.concatenate([derivs[0], derivs[1], derivs[2]], axis=0))
    tested = jnp.concatenate([back[1, :, 0:256], back[0, :, 0:256]], axis=1)
    grads[1] = dot(tested, jnp.concatenate([derivs[1], derivs[3]], axis=0))

    @pl.when(has_above)
    def _():
        down_stress.wait_recv()

    higher = laid_out([str_above[g] for g in range(3)])
    for k in range(12):
        mine = s_nodes[0, k].astype(F32)
        s_nodes[1, k] = window(
            [
                jnp.where(
                    first, shifted(higher[k // 4][c], -(k % 4)), mine[GROUP * c : GROUP * (c + 1)]
                )
                for c in range(3)
            ]
        )
    both = jnp.concatenate([stress_window(1, 0), stress_window(1, 1)], axis=0)
    at = dot(jnp.concatenate([ahead[4], ahead[4]], axis=1), both).astype(BF16)
    into(dflux.at[pl.ds(0, 768)], [at[:, column(c)] for c in range(6)])
    upper = dot(back[1, :, 256:], dflux[0:768])

    @pl.when(has_below)
    def _():
        up_share.wait_recv()

    from_below = cup_recv[...].astype(F32)[0:GROUP]
    for i in range(3):
        even, odd = around(upper, i)
        arrived = shifted(from_below, -i)
        shares[GROUP * 2 * i : GROUP * (2 * i + 1)] += jnp.where(first, arrived[:, 0:LANES], even)
        shares[GROUP * (2 * i + 1) : GROUP * (2 * i + 2)] += jnp.where(first, arrived[:, LANES:], odd)
    for k in range(8):
        rs_send[k] = raised(shares[56 * k : 56 * (k + 1)], 64)

    def share_copy(off):
        peer = lax.rem(mode + off, modes)
        return remote(
            rs_send.at[peer], rs_recv.at[off], rs_ssem.at[off], rs_rsem.at[off], (dom, peer)
        )

    for off in range(1, modes):
        share_copy(off).start()

    arrived_here(9)
    start_mass = jnp.where(first, jnp.where(has_below, 1.0, 2.0).astype(F32), jnp.ones((GROUP, LANES), F32))
    end_mass = jnp.where(has_above, 1.0, 0.0).astype(F32)

    def project(j, _):
        for i in range(3):
            cols = pl.ds(pl.multiple_of((3 * j + i) * LANES, LANES), LANES)
            mine, over = [], []
            for c in range(3):
                rows = slice(GROUP * c, GROUP * (c + 1))
                mine.append(grads[0, rows, cols])
                over.append(grads[1, rows, cols])
            results = []
            for parts, scale in ((mine, start_mass), (over, end_mass)):
                even = (parts[0] + pltpu.roll(parts[2], 1, axis=1)) * (inv_mass[0] * scale)
                odd = parts[1] * (inv_mass[1] * scale)
                results.append([even, odd, pltpu.roll(even, LANES - 1, axis=1)])
            p_nodes[0, 3 * i + j] = window(results[0])
            p_nodes[1, 3 * i + j] = window(
                [jnp.where(first, results[1][c], results[0][c]) for c in range(3)]
            )
        return 0

    lax.fori_loop(0, 3, project, 0)

    def projected_points(layer):
        for i in range(3):
            nodes = jnp.concatenate([p_nodes[layer, 3 * i + j] for j in range(3)], axis=1)
            here = dot(ahead[4 * layer], nodes)
            for j in range(3):
                g_points[layer, 3 * i + j] = here[:, column(j)]

    projected_points(1)
    velocity_points(1, dot(ahead[4], side(v_nodes, 1, 3)))

    def residual_of(layer, m, following):
        lam = jnp.full((16, LANES), relax[2 * mode + m], F32)
        eta = jnp.full((16, LANES), viscosity[2 * mode + m], F32)
        eps = jnp.full((16, LANES), extension[2 * mode + m], F32)
        half = 0.5 / lam
        slope = 0.5 * eps / eta
        kappa = eta / lam

        def chunk(start):
            rows = pl.ds(start, 16)
            t = [t_points[layer, m, 0, rows, column(c)] for c in range(6)]
            g = [[g_points[layer, 3 * i + j, rows] for j in range(3)] for i in range(3)]
            u = [flow[layer, i, rows] for i in range(3)]
            y = half + slope * (t[0] + t[1] + t[2])
            shift = (y * kappa) * 2.0
            tt = [t[0] + kappa, t[1] + kappa, t[2] + kappa] + t[3:]
            h = [g[k][k] - y for k in range(3)]

            def entry(i, j):
                return tt[SLOT[i][j]]

            for c, (i, j) in enumerate(((0, 0), (1, 1), (2, 2), (0, 1), (0, 2), (1, 2))):
                value = u[0] * t_points[layer, m, 1, rows, column(c)]
                value = value + u[1] * t_points[layer, m, 2, rows, column(c)]
                value = value + u[2] * t_points[layer, m, 3, rows, column(c)]
                if i == j:
                    k, l = (i + 1) % 3, (i + 2) % 3
                    part = h[i] * entry(i, i) + g[i][k] * entry(k, i) + g[i][l] * entry(l, i)
                    value = value - (part + part) - shift
                else:
                    k = 3 - i - j
                    part = (h[i] + h[j]) * entry(i, j)
                    part = part + g[i][j] * entry(j, j) + g[i][k] * entry(k, j)
                    part = part + g[j][i] * entry(i, i) + g[j][k] * entry(k, i)
                    value = value - part
                rounded = value.astype(BF16)
                flux[rows, column(c)] = rounded
                for j2 in range(3):
                    place = pl.ds(256 * (1 + j2) + start, 16)
                    flux[place, column(c)] = rounded * winds[layer, j2, rows]

        def step(k, _):
            chunk(pl.multiple_of(16 * k, 16))
            return 0

        bounds = (0, 4, 8, 11, 14)
        for d in range(4):
            lax.fori_loop(bounds[d], bounds[d + 1], step, 0, unroll=True)
            if following is not None:
                points_of(*following, d)
        sums[layer, m] = dot(back[layer], flux[...])

    weight = viscosity[0]
    for k in range(1, 2 * modes):
        weight = weight + viscosity[k]
    weight = weight * (1.0 / (2 * modes))

    def devss_of(layer):
        values = [None] * 6
        for i in range(3):
            for j in range(i, 3):
                d_ij = derivs[layer, 0:POINTS, column(3 * j + i)].astype(F32)
                d_ji = derivs[layer, 0:POINTS, column(3 * i + j)].astype(F32)
                excess = d_ij + d_ji - g_points[layer, 3 * i + j] - g_points[layer, 3 * j + i]
                values[SLOT[i][j]] = (weight * excess).astype(BF16)
        into(dflux.at[pl.ds(0, 768)], values)
        devss[layer] = dot(back[layer, :, 256:], dflux[0:768])

    tops = [
        remote(top_send.at[k], top_recv.at[k], top_ssem.at[k], top_rsem.at[k], above) for k in range(4)
    ]

    for d in range(4):
        points_of(1, 0, d)
    devss_of(1)
    for m in range(2):
        residual_of(1, m, ((1, 1), (0, 0))[m])
        result = sums[1, m]
        blocks = [jnp.concatenate(around(result, c), axis=1) for c in range(6)]
        result = devss[1]
        for i in ((0, 1), (2,))[m]:
            blocks.append(jnp.concatenate(around(result, i), axis=1))
        top_send[2 * m] = raised(packed(blocks[0:4]), SENT)
        top_send[2 * m + 1] = raised(packed(blocks[4:]), SENT)

        @pl.when(has_above)
        def _():
            tops[2 * m].start()
            tops[2 * m + 1].start()

    def sum_shares():
        place = pl.ds(pl.multiple_of(mode * 56, 8), 56)
        total = jnp.concatenate([shares[place], jnp.zeros((8, LANES), F32)], axis=0)
        for off in range(1, modes):
            share_copy(off).wait_recv()
            total = total + rs_recv[off].astype(F32)
        ag_buf[mode] = total.astype(BF16)

    def whole_copy(off, place):
        peer = lax.rem(mode + off, modes)
        return remote(
            ag_buf.at[place], ag_buf.at[place], ag_ssem.at[off], ag_rsem.at[off], (dom, peer)
        )

    sum_shares()
    for off in range(1, modes):
        whole_copy(off, mode).start()

    projected_points(0)
    devss_of(0)
    for m in range(2):
        residual_of(0, m, ((0, 1), None)[m])

    @pl.when(has_below)
    def _():
        for k in range(4):
            tops[k].wait_recv()

    def nodes_of(lower, upper, c, arrived):
        low = jnp.concatenate(around(lower, c), axis=1)
        high = jnp.concatenate(around(upper, c), axis=1)
        return low + jnp.where(firsts, arrived, high)

    def finish(m, _):
        lam = relax[2 * mode + m]
        lower, upper = sums[0, m], sums[1, m]
        arrived = [top_recv[2 * m + k].astype(F32)[0:GROUP] for k in range(2)]
        for c in range(6):
            both = nodes_of(lower, upper, c, shifted(arrived[c // 4], -(c % 4)))
            pieces[6 * m + c] = raised(both * lam, SENT)
        return 0

    lax.fori_loop(0, 2, finish, 0)

    for off in range(1, modes):
        whole_copy(off, lax.rem(mode + modes - off, modes)).wait_recv()

    for k in range(8):
        shares[56 * k : 56 * (k + 1)] = ag_buf[k].astype(F32)[0:56]
    lower, upper = devss[0], devss[1]
    for i in range(3):
        group, place = ((1, 2), (1, 3), (3, 2))[i]
        arrived = shifted(top_recv[group].astype(F32)[0:GROUP], -place)
        both = nodes_of(lower, upper, i, arrived)
        both = both + jnp.concatenate(
            [
                shares[GROUP * 2 * i : GROUP * (2 * i + 1)],
                shares[GROUP * (2 * i + 1) : GROUP * (2 * i + 2)],
            ],
            axis=1,
        )
        rounded = both.astype(BF16).astype(F32)
        pieces[12 + i] = raised(rounded, SENT)
        pieces[15 + i] = raised(both - rounded, SENT)

    @pl.when(has_below)
    def _():
        down_velocity.wait_send()
        down_stress.wait_send()

    @pl.when(has_above)
    def _():
        up_velocity.wait_send()
        up_share.wait_send()
        for k in range(4):
            tops[k].wait_send()

    for off in range(1, modes):
        share_copy(off).wait_send()
        whole_copy(off, mode).wait_send()


def finish_kernel(pieces, merge, out_stress, out_div, stress_rows, div_rows, sem):
    def merged(first):
        rows = dot(jnp.concatenate([pieces[first + k] for k in range(3)], axis=0), merge[...])
        return [
            rows[SENT * k : SENT * k + OWN * NODES].reshape(NODES, OWN, 2 * LANES) for k in range(3)
        ]

    copies = []
    for g in range(4):
        place = (g // 2, pl.ds(3 * (g % 2), 3))
        for k, rows in enumerate(merged(3 * g)):
            stress_rows[g // 2, 3 * (g % 2) + k] = rows.astype(BF16)
        copies.append(pltpu.make_async_copy(stress_rows.at[place], out_stress.at[place], sem.at[g]))
        copies[g].start()
    for k, (high, low) in enumerate(zip(merged(12), merged(15))):
        div_rows[k] = high + low
    copies.append(pltpu.make_async_copy(div_rows, out_div, sem.at[4]))
    copies[4].start()
    for copy in copies:
        copy.wait()


def on_device(doms, modes, velocity, stress, relax_time, viscosity, extensibility):
    ahead, back = column_tables()
    split, merge = order_tables()
    velocity = jnp.transpose(velocity, (0, 2, 1, 3))
    stress = jnp.transpose(stress, (0, 1, 3, 2, 4))
    vmem = pl.BlockSpec(memory_space=pltpu.VMEM)
    smem = pl.BlockSpec(memory_space=pltpu.SMEM)
    hbm = pl.BlockSpec(memory_space=pltpu.HBM)
    dma = pltpu.SemaphoreType.DMA
    around_nodes = 2 * LANES
    scratch = [
        pltpu.VMEM(velocity.shape, BF16),
        pltpu.VMEM(stress.shape, BF16),
        pltpu.VMEM(ahead.shape, BF16),
        pltpu.VMEM(back.shape, BF16),
        pltpu.VMEM(split.shape, BF16),
        pltpu.VMEM((2, GROUP, LANES), F32),
        pltpu.VMEM((12, SENT, around_nodes), BF16),
        pltpu.VMEM((3, SENT, around_nodes), BF16),
        pltpu.VMEM(velocity.shape, BF16),
        pltpu.VMEM(velocity.shape, BF16),
        pltpu.VMEM((3, SENT, around_nodes), BF16),
        pltpu.VMEM((SENT, around_nodes), BF16),
        pltpu.VMEM((SENT, around_nodes), BF16),
        pltpu.VMEM((4, SENT, around_nodes), BF16),
        pltpu.VMEM((4, SENT, around_nodes), BF16),
        pltpu.VMEM((2, 12, WINDOW, LANES), BF16),
        pltpu.VMEM((4, 3, WINDOW, LANES), BF16),
        pltpu.VMEM((2, 9, WINDOW, LANES), BF16),
        pltpu.VMEM((2, 2, 4, POINTS, 6 * LANES), F32),
        pltpu.VMEM((4 * 256, 6 * LANES), BF16),
        pltpu.VMEM((9 * 256, 3 * LANES), BF16),
        pltpu.VMEM((2, COLUMN, 4 * 256), F32),
        pltpu.VMEM((4, 256, 9 * LANES), BF16),
        pltpu.VMEM((2, COLUMN, 9 * LANES), F32),
        pltpu.VMEM((2, 3, POINTS, LANES), F32),
        pltpu.VMEM((2, 3, POINTS, LANES), BF16),
        pltpu.VMEM((2, 9, POINTS, LANES), F32),
        pltpu.VMEM((2, 2, COLUMN, 6 * LANES), F32),
        pltpu.VMEM((2, COLUMN, 3 * LANES), F32),
        pltpu.VMEM((448, LANES), F32),
        pltpu.VMEM((8, 64, LANES), BF16),
        pltpu.VMEM((8, 64, LANES), BF16),
        pltpu.VMEM((8, 64, LANES), BF16),
        dma((10,)),
        dma((4,)),
        dma((4,)),
        dma((modes,)),
        dma((modes,)),
        dma((modes,)),
        dma((modes,)),
        dma((4,)),
        dma((4,)),
    ]
    pieces = pl.pallas_call(
        functools.partial(kernel, doms, modes),
        out_shape=pltpu.VMEM((18, SENT, around_nodes), BF16),
        in_specs=[hbm, hbm, smem, smem, smem, hbm, hbm, hbm, hbm],
        out_specs=vmem,
        scratch_shapes=scratch,
        compiler_params=pltpu.CompilerParams(
            collective_id=0, has_side_effects=True, vmem_limit_bytes=58 * 1024 * 1024
        ),
        name="ptt",
    )(
        velocity,
        stress,
        relax_time,
        viscosity,
        extensibility,
        jnp.asarray(ahead),
        jnp.asarray(back),
        jnp.asarray(split),
        jnp.asarray(inverse_mass()),
    )
    out_stress, out_div = pl.pallas_call(
        finish_kernel,
        out_shape=(
            jax.ShapeDtypeStruct(stress.shape, BF16),
            jax.ShapeDtypeStruct(velocity.shape, F32),
        ),
        in_specs=[vmem, vmem],
        out_specs=(hbm, hbm),
        scratch_shapes=[pltpu.VMEM(stress.shape, BF16), pltpu.VMEM(velocity.shape, F32), dma((5,))],
        compiler_params=pltpu.CompilerParams(vmem_limit_bytes=16 * 1024 * 1024),
        name="finish",
    )(pieces, jnp.asarray(merge))
    return jnp.transpose(out_stress, (0, 1, 3, 2, 4)), jnp.transpose(out_div, (0, 2, 1, 3))


def solution(mesh):
    return jax.shard_map(
        functools.partial(on_device, mesh.shape["dom"], mesh.shape["mode"]),
        mesh=mesh,
        in_specs=(P(None, "dom", None, None), P("mode", None, "dom", None, None), P(), P(), P()),
        out_specs=(P("mode", None, "dom", None, None), P(None, "dom", None, None)),
        check_vma=False,
    )
```

```python
import functools

import jax
import jax.numpy as jnp
import ml_dtypes
import numpy as np
from jax import lax
from jax.experimental import pallas as pl
from jax.experimental.pallas import tpu as pltpu
from jax.sharding import PartitionSpec as P

F32 = jnp.float32
BF16 = jnp.bfloat16
MESH = pl.DeviceIdType.MESH
SLOT = ((0, 3, 4), (3, 1, 5), (4, 5, 2))
NODES = 17
OWN = 4
GROUP = 72
SENT = 80
COLUMN = 216
WINDOW = 256
POINTS = 224
LANES = 128


def gauss_tables():
    s = np.array([0.5 - 0.5 * np.sqrt(0.6), 0.5, 0.5 + 0.5 * np.sqrt(0.6)])
    weight = np.array([5.0, 8.0, 5.0]) / 18.0
    value = np.stack([2.0 * s * s - 3.0 * s + 1.0, 4.0 * s * (1.0 - s), 2.0 * s * s - s], axis=1)
    slope = np.stack([4.0 * s - 3.0, 4.0 - 8.0 * s, 4.0 * s - 1.0], axis=1)

    def product(first, second, third):
        joined = (
            first[:, None, None, :, None, None]
            * second[None, :, None, None, :, None]
            * third[None, None, :, None, None, :]
        )
        return joined.reshape(27, 27)

    forward = np.concatenate(
        [
            product(value, value, value),
            product(slope, value, value),
            product(value, slope, value),
            product(value, value, slope),
        ],
        axis=0,
    )
    volume = (weight[:, None, None] * weight[None, :, None] * weight[None, None, :]).reshape(27)
    testing = (forward * np.tile(volume, 4)[:, None]).T
    return forward.astype(ml_dtypes.bfloat16), testing.astype(ml_dtypes.bfloat16)


def column_tables():
    forward, testing = (np.asarray(t, np.float32) for t in gauss_tables())
    ahead = np.zeros((2, 4, POINTS, WINDOW), np.float32)
    back = np.zeros((2, COLUMN, 4 * 256), np.float32)
    for layer, slots in enumerate(((0, 1, 2), (2, 3, 0))):
        for f in range((NODES - 1) // 2):
            for n in range(27):
                a, b, c = n // 9, (n // 3) % 3, n % 3
                node = GROUP * c + OWN * (2 * f + b) + slots[a]
                for d in range(4):
                    rows = slice(27 * d, 27 * d + 27)
                    ahead[layer, d, 27 * f : 27 * f + 27, node] = forward[rows, n]
                    back[layer, node, 256 * d + 27 * f : 256 * d + 27 * f + 27] = testing[n, rows]
    ahead = ahead.reshape(8, POINTS, WINDOW)
    return ahead.astype(ml_dtypes.bfloat16), back.astype(ml_dtypes.bfloat16)


def order_tables():
    split = np.zeros((2 * LANES, 3 * LANES), np.float32)
    for g in range(LANES):
        split[2 * g, g] = 1.0
        split[2 * g + 1, LANES + g] = 1.0
        split[(2 * g + 2) % (2 * LANES), 2 * LANES + g] = 1.0
    merge = split[:, : 2 * LANES].T.copy()
    return split.astype(ml_dtypes.bfloat16), merge.astype(ml_dtypes.bfloat16)


def inverse_mass():
    r = np.arange(GROUP) // OWN
    mz = np.where(np.arange(GROUP) % 2 == 1, 2.0 / 3.0, 1.0 / 3.0)
    mr = np.where(r % 2 == 1, 2.0 / 3.0, np.where((r == 0) | (r >= NODES - 1), 1.0 / 6.0, 1.0 / 3.0))
    both = np.stack([3.0 / (mz * mr), 1.5 / (mz * mr)])
    return np.ascontiguousarray(np.broadcast_to(both[:, :, None], (2, GROUP, LANES))).astype(np.float32)


def dot(x, y):
    return jnp.dot(x, y, preferred_element_type=F32)


def raised(x, height):
    return jnp.concatenate([x, jnp.zeros((height - x.shape[0], x.shape[1]), F32)], axis=0).astype(BF16)


def column(c):
    return slice(LANES * c, LANES * (c + 1))


def kernel(
    doms,
    modes,
    velocity_hbm,
    stress_hbm,
    relax,
    viscosity,
    extension,
    ahead_hbm,
    back_hbm,
    split_hbm,
    mass_hbm,
    pieces,
    velocity,
    stress,
    ahead,
    back,
    split,
    inv_mass,
    s_rows,
    str_down,
    vel_above,
    vel_below,
    str_above,
    cup_send,
    cup_recv,
    top_send,
    top_recv,
    s_nodes,
    v_nodes,
    p_nodes,
    t_points,
    flux,
    dflux,
    masked,
    derivs,
    grads,
    flow,
    winds,
    g_points,
    sums,
    devss,
    shares,
    rs_send,
    rs_recv,
    ag_buf,
    local_sem,
    halo_send,
    halo_recv,
    rs_ssem,
    rs_rsem,
    ag_ssem,
    ag_rsem,
    top_ssem,
    top_rsem,
):
    dom = lax.axis_index("dom")
    mode = lax.axis_index("mode")
    has_below = dom > 0
    has_above = dom < doms - 1
    below = (jnp.maximum(dom - 1, 0), mode)
    above = (jnp.minimum(dom + 1, doms - 1), mode)
    inside = jnp.where(has_below, 1.0, 0.0).astype(F32)

    barrier = pltpu.get_barrier_semaphore()

    @pl.when(has_below)
    def _():
        pl.semaphore_signal(barrier, inc=1, device_id=below, device_id_type=MESH)

    @pl.when(has_above)
    def _():
        pl.semaphore_signal(barrier, inc=1, device_id=above, device_id_type=MESH)

    for off in range(1, modes):
        peer = lax.rem(mode + off, modes)
        pl.semaphore_signal(barrier, inc=1, device_id=(dom, peer), device_id_type=MESH)

    pairs = (
        (stress_hbm.at[0], stress.at[0]),
        (stress_hbm.at[1], stress.at[1]),
        (split_hbm, split),
        (ahead_hbm.at[0], ahead.at[0]),
        (ahead_hbm.at[4], ahead.at[4]),
        (back_hbm.at[1], back.at[1]),
        (back_hbm.at[0], back.at[0]),
        (velocity_hbm, velocity),
        (ahead_hbm.at[pl.ds(1, 3)], ahead.at[pl.ds(1, 3)]),
        (ahead_hbm.at[pl.ds(5, 3)], ahead.at[pl.ds(5, 3)]),
        (mass_hbm, inv_mass),
    )
    loads = [pltpu.make_async_copy(a, b, local_sem.at[k]) for k, (a, b) in enumerate(pairs)]

    def arrived_here(*which):
        for k in which:
            loads[k].wait()

    for load in loads:
        load.start()

    def remote(src, dst, send, recv, target):
        return pltpu.make_async_remote_copy(
            src_ref=src,
            dst_ref=dst,
            send_sem=send,
            recv_sem=recv,
            device_id=target,
            device_id_type=MESH,
        )

    down_velocity = remote(velocity_hbm, vel_above, halo_send.at[0], halo_recv.at[0], below)
    down_stress = remote(str_down, str_above, halo_send.at[1], halo_recv.at[1], below)
    up_velocity = remote(velocity_hbm, vel_below, halo_send.at[2], halo_recv.at[2], above)
    up_share = remote(cup_send, cup_recv, halo_send.at[3], halo_recv.at[3], above)

    @pl.when(jnp.logical_not(has_above))
    def _():
        vel_above[...] = jnp.zeros_like(vel_above)
        str_above[...] = jnp.zeros_like(str_above)

    @pl.when(jnp.logical_not(has_below))
    def _():
        vel_below[...] = jnp.zeros_like(vel_below)
        cup_recv[...] = jnp.zeros_like(cup_recv)
        top_recv[...] = jnp.zeros_like(top_recv)

    slot = lax.rem(lax.broadcasted_iota(jnp.int32, (GROUP, LANES), 0), OWN)
    slots = jnp.concatenate([slot, slot], axis=1)
    first = slot == 0
    firsts = slots == 0

    def shifted(block, rows):
        return block if rows == 0 else pltpu.roll(block, rows % GROUP, axis=0)

    def packed(blocks):
        result = blocks[0]
        for q in range(1, len(blocks)):
            result = jnp.where(slots == q, shifted(blocks[q], q), result)
        return result

    def rows_of(ref):
        return jnp.concatenate(
            [ref.astype(F32).reshape(OWN * NODES, 2 * LANES), jnp.zeros((GROUP - OWN * NODES, 2 * LANES), F32)],
            axis=0,
        )

    arrived_here(0, 1)
    for g in range(3):
        blocks = []
        for q in range(4):
            k = 4 * g + q
            blocks.append(rows_of(stress[k // 6, k % 6]))
            s_rows[k] = raised(blocks[q], SENT)
        str_down[g] = raised(packed(blocks), SENT)

    def laid_out(rows):
        spread = dot(jnp.concatenate(rows, axis=0), split[...])
        return [
            [spread[SENT * k : SENT * k + GROUP, column(c)] for c in range(3)] for k in range(len(rows))
        ]

    def window(parts):
        return raised(jnp.concatenate(parts, axis=0), WINDOW)

    for d in range(4):
        flux[256 * d + POINTS : 256 * (d + 1)] = jnp.zeros((256 - POINTS, 6 * LANES), BF16)
        derivs[d, POINTS:] = jnp.zeros((256 - POINTS, 9 * LANES), BF16)
    for d in range(9):
        dflux[256 * d + POINTS : 256 * (d + 1)] = jnp.zeros((256 - POINTS, 3 * LANES), BF16)

    arrived_here(2)
    for k in range(4):
        own = laid_out([s_rows[3 * k + c] for c in range(3)])
        for c in range(3):
            s_nodes[0, 3 * k + c] = window(own[c])

    def side(ref, index, count):
        return jnp.concatenate([ref[index, c] for c in range(count)], axis=1)

    def stress_window(layer, m):
        return jnp.concatenate([s_nodes[layer, 6 * m + c] for c in range(6)], axis=1)

    def around(result, c):
        even = result[0:GROUP, column(c)] + pltpu.roll(result[2 * GROUP :, column(c)], 1, axis=1)
        return even, result[GROUP : 2 * GROUP, column(c)]

    def points_of(layer, m, d):
        t_points[layer, m, d] = dot(ahead[4 * layer + d], stress_window(layer, m))

    def into(ref, values):
        for j in range(3):
            for i in range(3):
                ref[256 * j : 256 * j + POINTS, column(i)] = values[SLOT[i][j]]

    others = modes - 1 + has_below.astype(jnp.int32) + has_above.astype(jnp.int32)
    pl.semaphore_wait(barrier, others)

    @pl.when(has_below)
    def _():
        down_velocity.start()

    @pl.when(has_above)
    def _():
        up_velocity.start()

    @pl.when(has_below)
    def _():
        down_stress.start()

    arrived_here(3, 4, 5, 6)
    both = jnp.concatenate([stress_window(0, 0), stress_window(0, 1)], axis=0)
    upper = ahead[4].astype(F32)
    lane = lax.rem(lax.broadcasted_iota(jnp.int32, (POINTS, WINDOW), 1), OWN)
    zero = jnp.zeros_like(upper)
    parts = jnp.concatenate(
        [
            jnp.where(lane == 0, zero, upper).astype(BF16),
            jnp.where(lane == 0, upper, zero).astype(BF16),
            ahead[0],
        ],
        axis=0,
    )
    at = dot(jnp.concatenate([parts, parts], axis=1), both)
    for part in range(3):
        here = at[POINTS * part : POINTS * (part + 1)]
        if part == 1:
            here = here * inside
        here = here.astype(BF16)
        into(dflux.at[pl.ds(768 * part, 768)], [here[:, column(c)] for c in range(6)])
    outer = dot(back[1, :, 256:], dflux[0:768])
    for k in range(3):
        rows = slice(GROUP * k, GROUP * (k + 1))
        own = back[1, rows].astype(F32)
        zero = jnp.zeros_like(own)
        is_first = jnp.concatenate([first] * 8, axis=1)
        masked[0, rows] = jnp.where(is_first, own, zero)
        masked[1, rows] = jnp.where(is_first, zero, own[:, 0:1024])
    tested = jnp.concatenate([masked[0, :, 256:].astype(BF16), back[0, :, 256:]], axis=1)
    local = dot(tested, dflux[768:])
    cup_send[...] = raised(packed([jnp.concatenate(around(outer, i), axis=1) for i in range(3)]), SENT)

    @pl.when(has_above)
    def _():
        up_share.start()

    for i in range(3):
        even, odd = around(local, i)
        shares[GROUP * 2 * i : GROUP * (2 * i + 1)] = even
        shares[GROUP * (2 * i + 1) : GROUP * (2 * i + 2)] = odd

    def velocity_points(layer, at):
        at = at.astype(BF16).astype(F32)
        u = [at[:, column(i)] for i in range(3)]
        upwind = 0.5 / (1.0 + jnp.sqrt(u[0] * u[0] + u[1] * u[1] + u[2] * u[2]))
        for i in range(3):
            flow[layer, i] = u[i]
            winds[layer, i] = (upwind * u[i]).astype(BF16)

    def gradient_points(variant, layer):
        nodes = side(v_nodes, variant, 3)
        for j in range(3):
            at = dot(ahead[4 * layer + 1 + j], nodes)
            derivs[variant, 0:POINTS, 3 * LANES * j : 3 * LANES * (j + 1)] = at.astype(BF16)

    arrived_here(7, 8)
    own_velocity = laid_out([raised(rows_of(velocity[i]), SENT) for i in range(3)])
    for i in range(3):
        v_nodes[0, i] = window(own_velocity[i])

    velocity_points(0, dot(ahead[0], side(v_nodes, 0, 3)))
    gradient_points(0, 0)

    @pl.when(has_above)
    def _():
        down_velocity.wait_recv()

    @pl.when(has_below)
    def _():
        up_velocity.wait_recv()

    six = laid_out([raised(rows_of(ref[i]), SENT) for ref in (vel_above, vel_below) for i in range(3)])
    higher, lower = six[0:3], six[3:6]
    own = [
        [v_nodes[0, i, 0:224].astype(F32)[GROUP * c : GROUP * (c + 1)] for c in range(3)]
        for i in range(3)
    ]
    for i in range(3):
        v_nodes[1, i] = window([jnp.where(first, higher[i][c], own[i][c]) for c in range(3)])
        v_nodes[2, i] = window([jnp.where(first, own[i][c] * inside, lower[i][c]) for c in range(3)])
        v_nodes[3, i] = window(higher[i])
    arrived_here(9)
    gradient_points(1, 1)
    gradient_points(2, 1)
    gradient_points(3, 0)
    tested = jnp.concatenate(
        [back[0, :, 0:256], masked[1, :, 0:256].astype(BF16), masked[0, :, 0:256].astype(BF16)], axis=1
    )
    grads[0] = dot(tested, jnp.concatenate([derivs[0], derivs[1], derivs[2]], axis=0))
    tested = jnp.concatenate([back[1, :, 0:256], back[0, :, 0:256]], axis=1)
    grads[1] = dot(tested, jnp.concatenate([derivs[1], derivs[3]], axis=0))

    @pl.when(has_above)
    def _():
        down_stress.wait_recv()

    higher = laid_out([str_above[g] for g in range(3)])
    for k in range(12):
        mine = s_nodes[0, k].astype(F32)
        s_nodes[1, k] = window(
            [
                jnp.where(
                    first, shifted(higher[k // 4][c], -(k % 4)), mine[GROUP * c : GROUP * (c + 1)]
                )
                for c in range(3)
            ]
        )
    both = jnp.concatenate([stress_window(1, 0), stress_window(1, 1)], axis=0)
    at = dot(jnp.concatenate([ahead[4], ahead[4]], axis=1), both).astype(BF16)
    into(dflux.at[pl.ds(0, 768)], [at[:, column(c)] for c in range(6)])
    upper = dot(back[1, :, 256:], dflux[0:768])

    @pl.when(has_below)
    def _():
        up_share.wait_recv()

    from_below = cup_recv[...].astype(F32)[0:GROUP]
    for i in range(3):
        even, odd = around(upper, i)
        arrived = shifted(from_below, -i)
        shares[GROUP * 2 * i : GROUP * (2 * i + 1)] += jnp.where(first, arrived[:, 0:LANES], even)
        shares[GROUP * (2 * i + 1) : GROUP * (2 * i + 2)] += jnp.where(first, arrived[:, LANES:], odd)
    for k in range(8):
        rs_send[k] = raised(shares[56 * k : 56 * (k + 1)], 64)

    def share_copy(off):
        peer = lax.rem(mode + off, modes)
        return remote(
            rs_send.at[peer], rs_recv.at[off], rs_ssem.at[off], rs_rsem.at[off], (dom, peer)
        )

    for off in range(1, modes):
        share_copy(off).start()

    arrived_here(10)
    start_mass = jnp.where(first, jnp.where(has_below, 1.0, 2.0).astype(F32), jnp.ones((GROUP, LANES), F32))
    end_mass = jnp.where(has_above, 1.0, 0.0).astype(F32)

    def project(j, _):
        for i in range(3):
            cols = pl.ds(pl.multiple_of((3 * j + i) * LANES, LANES), LANES)
            mine, over = [], []
            for c in range(3):
                rows = slice(GROUP * c, GROUP * (c + 1))
                mine.append(grads[0, rows, cols])
                over.append(grads[1, rows, cols])
            results = []
            for parts, scale in ((mine, start_mass), (over, end_mass)):
                even = (parts[0] + pltpu.roll(parts[2], 1, axis=1)) * (inv_mass[0] * scale)
                odd = parts[1] * (inv_mass[1] * scale)
                results.append([even, odd, pltpu.roll(even, LANES - 1, axis=1)])
            p_nodes[0, 3 * i + j] = window(results[0])
            p_nodes[1, 3 * i + j] = window(
                [jnp.where(first, results[1][c], results[0][c]) for c in range(3)]
            )
        return 0

    lax.fori_loop(0, 3, project, 0)

    def projected_points(layer):
        for i in range(3):
            nodes = jnp.concatenate([p_nodes[layer, 3 * i + j] for j in range(3)], axis=1)
            here = dot(ahead[4 * layer], nodes)
            for j in range(3):
                g_points[layer, 3 * i + j] = here[:, column(j)]

    projected_points(1)
    velocity_points(1, dot(ahead[4], side(v_nodes, 1, 3)))

    def residual_of(layer, m, following):
        lam = jnp.full((16, LANES), relax[2 * mode + m], F32)
        eta = jnp.full((16, LANES), viscosity[2 * mode + m], F32)
        eps = jnp.full((16, LANES), extension[2 * mode + m], F32)
        half = 0.5 / lam
        slope = 0.5 * eps / eta
        kappa = eta / lam

        def chunk(start):
            rows = pl.ds(start, 16)
            t = [t_points[layer, m, 0, rows, column(c)] for c in range(6)]
            g = [[g_points[layer, 3 * i + j, rows] for j in range(3)] for i in range(3)]
            u = [flow[layer, i, rows] for i in range(3)]
            y = half + slope * (t[0] + t[1] + t[2])
            shift = (y * kappa) * 2.0
            tt = [t[0] + kappa, t[1] + kappa, t[2] + kappa] + t[3:]
            h = [g[k][k] - y for k in range(3)]

            def entry(i, j):
                return tt[SLOT[i][j]]

            for c, (i, j) in enumerate(((0, 0), (1, 1), (2, 2), (0, 1), (0, 2), (1, 2))):
                value = u[0] * t_points[layer, m, 1, rows, column(c)]
                value = value + u[1] * t_points[layer, m, 2, rows, column(c)]
                value = value + u[2] * t_points[layer, m, 3, rows, column(c)]
                if i == j:
                    k, l = (i + 1) % 3, (i + 2) % 3
                    part = h[i] * entry(i, i) + g[i][k] * entry(k, i) + g[i][l] * entry(l, i)
                    value = value - (part + part) - shift
                else:
                    k = 3 - i - j
                    part = (h[i] + h[j]) * entry(i, j)
                    part = part + g[i][j] * entry(j, j) + g[i][k] * entry(k, j)
                    part = part + g[j][i] * entry(i, i) + g[j][k] * entry(k, i)
                    value = value - part
                rounded = value.astype(BF16)
                flux[rows, column(c)] = rounded
                for j2 in range(3):
                    place = pl.ds(256 * (1 + j2) + start, 16)
                    flux[place, column(c)] = rounded * winds[layer, j2, rows]

        def step(k, _):
            chunk(pl.multiple_of(16 * k, 16))
            return 0

        bounds = (0, 4, 8, 11, 14)
        for d in range(4):
            lax.fori_loop(bounds[d], bounds[d + 1], step, 0, unroll=True)
            if following is not None:
                points_of(*following, d)
        sums[layer, m] = dot(back[layer], flux[...])

    weight = viscosity[0]
    for k in range(1, 2 * modes):
        weight = weight + viscosity[k]
    weight = weight * (1.0 / (2 * modes))

    def devss_of(layer):
        values = [None] * 6
        for i in range(3):
            for j in range(i, 3):
                d_ij = derivs[layer, 0:POINTS, column(3 * j + i)].astype(F32)
                d_ji = derivs[layer, 0:POINTS, column(3 * i + j)].astype(F32)
                excess = d_ij + d_ji - g_points[layer, 3 * i + j] - g_points[layer, 3 * j + i]
                values[SLOT[i][j]] = (weight * excess).astype(BF16)
        into(dflux.at[pl.ds(0, 768)], values)
        devss[layer] = dot(back[layer, :, 256:], dflux[0:768])

    tops = [
        remote(top_send.at[k], top_recv.at[k], top_ssem.at[k], top_rsem.at[k], above) for k in range(4)
    ]

    for d in range(4):
        points_of(1, 0, d)
    devss_of(1)
    for m in range(2):
        residual_of(1, m, ((1, 1), (0, 0))[m])
        result = sums[1, m]
        blocks = [jnp.concatenate(around(result, c), axis=1) for c in range(6)]
        result = devss[1]
        for i in ((0, 1), (2,))[m]:
            blocks.append(jnp.concatenate(around(result, i), axis=1))
        top_send[2 * m] = raised(packed(blocks[0:4]), SENT)
        top_send[2 * m + 1] = raised(packed(blocks[4:]), SENT)

        @pl.when(has_above)
        def _():
            tops[2 * m].start()
            tops[2 * m + 1].start()

    def sum_shares():
        place = pl.ds(pl.multiple_of(mode * 56, 8), 56)
        total = jnp.concatenate([shares[place], jnp.zeros((8, LANES), F32)], axis=0)
        for off in range(1, modes):
            share_copy(off).wait_recv()
            total = total + rs_recv[off].astype(F32)
        ag_buf[mode] = total.astype(BF16)

    def whole_copy(off, place):
        peer = lax.rem(mode + off, modes)
        return remote(
            ag_buf.at[place], ag_buf.at[place], ag_ssem.at[off], ag_rsem.at[off], (dom, peer)
        )

    sum_shares()
    for off in range(1, modes):
        whole_copy(off, mode).start()

    projected_points(0)
    devss_of(0)
    for m in range(2):
        residual_of(0, m, ((0, 1), None)[m])

    @pl.when(has_below)
    def _():
        for k in range(4):
            tops[k].wait_recv()

    def nodes_of(lower, upper, c, arrived):
        parts = []
        for k in range(3):
            rows = slice(GROUP * k, GROUP * (k + 1))
            high = upper[rows, column(c)]
            parts.append(lower[rows, column(c)] + jnp.where(first, jnp.zeros_like(high), high))
        even = parts[0] + pltpu.roll(parts[2], 1, axis=1)
        both = jnp.concatenate([even, parts[1]], axis=1)
        return both + jnp.where(firsts, arrived, jnp.zeros_like(both))

    def finish(m, _):
        lam = relax[2 * mode + m]
        lower, upper = sums[0, m], sums[1, m]
        arrived = [top_recv[2 * m + k].astype(F32)[0:GROUP] for k in range(2)]
        for c in range(6):
            both = nodes_of(lower, upper, c, shifted(arrived[c // 4], -(c % 4)))
            pieces[6 * m + c] = raised(both * lam, SENT)
        return 0

    lax.fori_loop(0, 2, finish, 0)

    for off in range(1, modes):
        whole_copy(off, lax.rem(mode + modes - off, modes)).wait_recv()

    for k in range(8):
        shares[56 * k : 56 * (k + 1)] = ag_buf[k].astype(F32)[0:56]
    lower, upper = devss[0], devss[1]
    for i in range(3):
        group, place = ((1, 2), (1, 3), (3, 2))[i]
        arrived = shifted(top_recv[group].astype(F32)[0:GROUP], -place)
        both = nodes_of(lower, upper, i, arrived)
        both = both + jnp.concatenate(
            [
                shares[GROUP * 2 * i : GROUP * (2 * i + 1)],
                shares[GROUP * (2 * i + 1) : GROUP * (2 * i + 2)],
            ],
            axis=1,
        )
        rounded = both.astype(BF16).astype(F32)
        pieces[12 + i] = raised(rounded, SENT)
        pieces[15 + i] = raised(both - rounded, SENT)

    @pl.when(has_below)
    def _():
        down_velocity.wait_send()
        down_stress.wait_send()

    @pl.when(has_above)
    def _():
        up_velocity.wait_send()
        up_share.wait_send()
        for k in range(4):
            tops[k].wait_send()

    for off in range(1, modes):
        share_copy(off).wait_send()
        whole_copy(off, mode).wait_send()


def finish_kernel(pieces, merge, out_stress, out_div, stress_rows, div_rows, sem):
    def merged(first):
        rows = dot(jnp.concatenate([pieces[first + k] for k in range(3)], axis=0), merge[...])
        return [
            rows[SENT * k : SENT * k + OWN * NODES].reshape(NODES, OWN, 2 * LANES) for k in range(3)
        ]

    copies = []
    for g in range(4):
        place = (g // 2, pl.ds(3 * (g % 2), 3))
        for k, rows in enumerate(merged(3 * g)):
            stress_rows[g // 2, 3 * (g % 2) + k] = rows.astype(BF16)
        copies.append(pltpu.make_async_copy(stress_rows.at[place], out_stress.at[place], sem.at[g]))
        copies[g].start()
    for k, (high, low) in enumerate(zip(merged(12), merged(15))):
        div_rows[k] = high + low
    copies.append(pltpu.make_async_copy(div_rows, out_div, sem.at[4]))
    copies[4].start()
    for copy in copies:
        copy.wait()


def on_device(doms, modes, velocity, stress, relax_time, viscosity, extensibility):
    ahead, back = column_tables()
    split, merge = order_tables()
    velocity = jnp.transpose(velocity, (0, 2, 1, 3))
    stress = jnp.transpose(stress, (0, 1, 3, 2, 4))
    vmem = pl.BlockSpec(memory_space=pltpu.VMEM)
    smem = pl.BlockSpec(memory_space=pltpu.SMEM)
    hbm = pl.BlockSpec(memory_space=pltpu.HBM)
    dma = pltpu.SemaphoreType.DMA
    around_nodes = 2 * LANES
    scratch = [
        pltpu.VMEM(velocity.shape, BF16),
        pltpu.VMEM(stress.shape, BF16),
        pltpu.VMEM(ahead.shape, BF16),
        pltpu.VMEM(back.shape, BF16),
        pltpu.VMEM(split.shape, BF16),
        pltpu.VMEM((2, GROUP, LANES), F32),
        pltpu.VMEM((12, SENT, around_nodes), BF16),
        pltpu.VMEM((3, SENT, around_nodes), BF16),
        pltpu.VMEM(velocity.shape, BF16),
        pltpu.VMEM(velocity.shape, BF16),
        pltpu.VMEM((3, SENT, around_nodes), BF16),
        pltpu.VMEM((SENT, around_nodes), BF16),
        pltpu.VMEM((SENT, around_nodes), BF16),
        pltpu.VMEM((4, SENT, around_nodes), BF16),
        pltpu.VMEM((4, SENT, around_nodes), BF16),
        pltpu.VMEM((2, 12, WINDOW, LANES), BF16),
        pltpu.VMEM((4, 3, WINDOW, LANES), BF16),
        pltpu.VMEM((2, 9, WINDOW, LANES), BF16),
        pltpu.VMEM((2, 2, 4, POINTS, 6 * LANES), F32),
        pltpu.VMEM((4 * 256, 6 * LANES), BF16),
        pltpu.VMEM((9 * 256, 3 * LANES), BF16),
        pltpu.VMEM((2, COLUMN, 4 * 256), F32),
        pltpu.VMEM((4, 256, 9 * LANES), BF16),
        pltpu.VMEM((2, COLUMN, 9 * LANES), F32),
        pltpu.VMEM((2, 3, POINTS, LANES), F32),
        pltpu.VMEM((2, 3, POINTS, LANES), BF16),
        pltpu.VMEM((2, 9, POINTS, LANES), F32),
        pltpu.VMEM((2, 2, COLUMN, 6 * LANES), F32),
        pltpu.VMEM((2, COLUMN, 3 * LANES), F32),
        pltpu.VMEM((448, LANES), F32),
        pltpu.VMEM((8, 64, LANES), BF16),
        pltpu.VMEM((8, 64, LANES), BF16),
        pltpu.VMEM((8, 64, LANES), BF16),
        dma((11,)),
        dma((4,)),
        dma((4,)),
        dma((modes,)),
        dma((modes,)),
        dma((modes,)),
        dma((modes,)),
        dma((4,)),
        dma((4,)),
    ]
    pieces = pl.pallas_call(
        functools.partial(kernel, doms, modes),
        out_shape=pltpu.VMEM((18, SENT, around_nodes), BF16),
        in_specs=[hbm, hbm, smem, smem, smem, hbm, hbm, hbm, hbm],
        out_specs=vmem,
        scratch_shapes=scratch,
        compiler_params=pltpu.CompilerParams(
            collective_id=0, has_side_effects=True, vmem_limit_bytes=58 * 1024 * 1024
        ),
        name="ptt",
    )(
        velocity,
        stress,
        relax_time,
        viscosity,
        extensibility,
        jnp.asarray(ahead),
        jnp.asarray(back),
        jnp.asarray(split),
        jnp.asarray(inverse_mass()),
    )
    out_stress, out_div = pl.pallas_call(
        finish_kernel,
        out_shape=(
            jax.ShapeDtypeStruct(stress.shape, BF16),
            jax.ShapeDtypeStruct(velocity.shape, F32),
        ),
        in_specs=[vmem, vmem],
        out_specs=(hbm, hbm),
        scratch_shapes=[pltpu.VMEM(stress.shape, BF16), pltpu.VMEM(velocity.shape, F32), dma((5,))],
        compiler_params=pltpu.CompilerParams(vmem_limit_bytes=16 * 1024 * 1024),
        name="finish",
    )(pieces, jnp.asarray(merge))
    return jnp.transpose(out_stress, (0, 1, 3, 2, 4)), jnp.transpose(out_div, (0, 2, 1, 3))


def solution(mesh):
    return jax.shard_map(
        functools.partial(on_device, mesh.shape["dom"], mesh.shape["mode"]),
        mesh=mesh,
        in_specs=(P(None, "dom", None, None), P("mode", None, "dom", None, None), P(), P(), P()),
        out_specs=(P("mode", None, "dom", None, None), P(None, "dom", None, None)),
        check_vma=False,
    )
```

```python
import functools

import jax
import jax.numpy as jnp
import ml_dtypes
import numpy as np
from jax import lax
from jax.experimental import pallas as pl
from jax.experimental.pallas import tpu as pltpu
from jax.sharding import PartitionSpec as P

F32 = jnp.float32
BF16 = jnp.bfloat16
MESH = pl.DeviceIdType.MESH
SLOT = ((0, 3, 4), (3, 1, 5), (4, 5, 2))
NODES = 17
OWN = 4
GROUP = 72
SENT = 80
COLUMN = 216
WINDOW = 256
POINTS = 224
LANES = 128


def gauss_tables():
    s = np.array([0.5 - 0.5 * np.sqrt(0.6), 0.5, 0.5 + 0.5 * np.sqrt(0.6)])
    weight = np.array([5.0, 8.0, 5.0]) / 18.0
    value = np.stack([2.0 * s * s - 3.0 * s + 1.0, 4.0 * s * (1.0 - s), 2.0 * s * s - s], axis=1)
    slope = np.stack([4.0 * s - 3.0, 4.0 - 8.0 * s, 4.0 * s - 1.0], axis=1)

    def product(first, second, third):
        joined = (
            first[:, None, None, :, None, None]
            * second[None, :, None, None, :, None]
            * third[None, None, :, None, None, :]
        )
        return joined.reshape(27, 27)

    forward = np.concatenate(
        [
            product(value, value, value),
            product(slope, value, value),
            product(value, slope, value),
            product(value, value, slope),
        ],
        axis=0,
    )
    volume = (weight[:, None, None] * weight[None, :, None] * weight[None, None, :]).reshape(27)
    testing = (forward * np.tile(volume, 4)[:, None]).T
    return forward.astype(ml_dtypes.bfloat16), testing.astype(ml_dtypes.bfloat16)


def column_tables():
    forward, testing = (np.asarray(t, np.float32) for t in gauss_tables())
    ahead = np.zeros((2, 4, POINTS, WINDOW), np.float32)
    back = np.zeros((2, COLUMN, 4 * 256), np.float32)
    for layer, slots in enumerate(((0, 1, 2), (2, 3, 0))):
        for f in range((NODES - 1) // 2):
            for n in range(27):
                a, b, c = n // 9, (n // 3) % 3, n % 3
                node = GROUP * c + OWN * (2 * f + b) + slots[a]
                for d in range(4):
                    rows = slice(27 * d, 27 * d + 27)
                    ahead[layer, d, 27 * f : 27 * f + 27, node] = forward[rows, n]
                    back[layer, node, 256 * d + 27 * f : 256 * d + 27 * f + 27] = testing[n, rows]
    ahead = ahead.reshape(8, POINTS, WINDOW)
    return ahead.astype(ml_dtypes.bfloat16), back.astype(ml_dtypes.bfloat16)


def order_tables():
    split = np.zeros((2 * LANES, 3 * LANES), np.float32)
    for g in range(LANES):
        split[2 * g, g] = 1.0
        split[2 * g + 1, LANES + g] = 1.0
        split[(2 * g + 2) % (2 * LANES), 2 * LANES + g] = 1.0
    merge = split[:, : 2 * LANES].T.copy()
    return split.astype(ml_dtypes.bfloat16), merge.astype(ml_dtypes.bfloat16)


def inverse_mass():
    r = np.arange(GROUP) // OWN
    mz = np.where(np.arange(GROUP) % 2 == 1, 2.0 / 3.0, 1.0 / 3.0)
    mr = np.where(r % 2 == 1, 2.0 / 3.0, np.where((r == 0) | (r >= NODES - 1), 1.0 / 6.0, 1.0 / 3.0))
    both = np.stack([3.0 / (mz * mr), 1.5 / (mz * mr)])
    return np.ascontiguousarray(np.broadcast_to(both[:, :, None], (2, GROUP, LANES))).astype(np.float32)


def dot(x, y):
    return jnp.dot(x, y, preferred_element_type=F32)


def raised(x, height):
    return jnp.concatenate([x, jnp.zeros((height - x.shape[0], x.shape[1]), F32)], axis=0).astype(BF16)


def column(c):
    return slice(LANES * c, LANES * (c + 1))


def kernel(
    doms,
    modes,
    velocity_hbm,
    stress_hbm,
    relax,
    viscosity,
    extension,
    ahead_hbm,
    back_hbm,
    split_hbm,
    mass_hbm,
    pieces,
    velocity,
    stress,
    ahead,
    back,
    split,
    inv_mass,
    s_rows,
    str_down,
    vel_up,
    vel_above,
    vel_below,
    str_above,
    cup_send,
    cup_recv,
    top_send,
    top_recv,
    s_nodes,
    v_nodes,
    p_nodes,
    t_points,
    flux,
    dflux,
    masked,
    derivs,
    grads,
    flow,
    winds,
    g_points,
    sums,
    devss,
    shares,
    rs_send,
    rs_recv,
    ag_buf,
    local_sem,
    halo_send,
    halo_recv,
    rs_ssem,
    rs_rsem,
    ag_ssem,
    ag_rsem,
    top_ssem,
    top_rsem,
):
    dom = lax.axis_index("dom")
    mode = lax.axis_index("mode")
    has_below = dom > 0
    has_above = dom < doms - 1
    below = (jnp.maximum(dom - 1, 0), mode)
    above = (jnp.minimum(dom + 1, doms - 1), mode)
    inside = jnp.where(has_below, 1.0, 0.0).astype(F32)

    barrier = pltpu.get_barrier_semaphore()

    @pl.when(has_below)
    def _():
        pl.semaphore_signal(barrier, inc=1, device_id=below, device_id_type=MESH)

    @pl.when(has_above)
    def _():
        pl.semaphore_signal(barrier, inc=1, device_id=above, device_id_type=MESH)

    for off in range(1, modes):
        peer = lax.rem(mode + off, modes)
        pl.semaphore_signal(barrier, inc=1, device_id=(dom, peer), device_id_type=MESH)

    pairs = (
        (velocity_hbm, velocity),
        (stress_hbm.at[0], stress.at[0]),
        (stress_hbm.at[1], stress.at[1]),
        (split_hbm, split),
        (ahead_hbm.at[0], ahead.at[0]),
        (ahead_hbm.at[4], ahead.at[4]),
        (back_hbm.at[1], back.at[1]),
        (back_hbm.at[0], back.at[0]),
        (ahead_hbm.at[pl.ds(1, 3)], ahead.at[pl.ds(1, 3)]),
        (ahead_hbm.at[pl.ds(5, 3)], ahead.at[pl.ds(5, 3)]),
        (mass_hbm, inv_mass),
    )
    loads = [pltpu.make_async_copy(a, b, local_sem.at[k]) for k, (a, b) in enumerate(pairs)]

    def arrived_here(*which):
        for k in which:
            loads[k].wait()

    for load in loads:
        load.start()

    def remote(src, dst, send, recv, target):
        return pltpu.make_async_remote_copy(
            src_ref=src,
            dst_ref=dst,
            send_sem=send,
            recv_sem=recv,
            device_id=target,
            device_id_type=MESH,
        )

    down_velocity = remote(velocity_hbm, vel_above, halo_send.at[0], halo_recv.at[0], below)
    down_stress = remote(str_down, str_above, halo_send.at[1], halo_recv.at[1], below)
    up_velocity = remote(vel_up, vel_below, halo_send.at[2], halo_recv.at[2], above)
    up_share = remote(cup_send, cup_recv, halo_send.at[3], halo_recv.at[3], above)

    @pl.when(jnp.logical_not(has_above))
    def _():
        vel_above[...] = jnp.zeros_like(vel_above)
        str_above[...] = jnp.zeros_like(str_above)

    @pl.when(jnp.logical_not(has_below))
    def _():
        vel_below[...] = jnp.zeros_like(vel_below)
        cup_recv[...] = jnp.zeros_like(cup_recv)
        top_recv[...] = jnp.zeros_like(top_recv)

    slot = lax.rem(lax.broadcasted_iota(jnp.int32, (GROUP, LANES), 0), OWN)
    slots = jnp.concatenate([slot, slot], axis=1)
    first = slot == 0
    firsts = slots == 0

    def shifted(block, rows):
        return block if rows == 0 else pltpu.roll(block, rows % GROUP, axis=0)

    def packed(blocks):
        result = blocks[0]
        for q in range(1, len(blocks)):
            result = jnp.where(slots == q, shifted(blocks[q], q), result)
        return result

    def rows_of(ref):
        return jnp.concatenate(
            [ref.astype(F32).reshape(OWN * NODES, 2 * LANES), jnp.zeros((GROUP - OWN * NODES, 2 * LANES), F32)],
            axis=0,
        )

    arrived_here(0)
    blocks = [rows_of(velocity[i]) for i in range(3)]
    vel_up[0] = raised(jnp.where(slots >= 2, blocks[0], shifted(blocks[1], -2)), SENT)
    vel_up[1] = raised(blocks[2], SENT)
    arrived_here(1, 2)
    for g in range(3):
        blocks = []
        for q in range(4):
            k = 4 * g + q
            blocks.append(rows_of(stress[k // 6, k % 6]))
            s_rows[k] = raised(blocks[q], SENT)
        str_down[g] = raised(packed(blocks), SENT)

    def laid_out(rows):
        spread = dot(jnp.concatenate(rows, axis=0), split[...])
        return [
            [spread[SENT * k : SENT * k + GROUP, column(c)] for c in range(3)] for k in range(len(rows))
        ]

    def window(parts):
        return raised(jnp.concatenate(parts, axis=0), WINDOW)

    for d in range(4):
        flux[256 * d + POINTS : 256 * (d + 1)] = jnp.zeros((256 - POINTS, 6 * LANES), BF16)
        derivs[d, POINTS:] = jnp.zeros((256 - POINTS, 9 * LANES), BF16)
    for d in range(9):
        dflux[256 * d + POINTS : 256 * (d + 1)] = jnp.zeros((256 - POINTS, 3 * LANES), BF16)

    arrived_here(3)
    for k in range(4):
        own = laid_out([s_rows[3 * k + c] for c in range(3)])
        for c in range(3):
            s_nodes[0, 3 * k + c] = window(own[c])

    def side(ref, index, count):
        return jnp.concatenate([ref[index, c] for c in range(count)], axis=1)

    def stress_window(layer, m):
        return jnp.concatenate([s_nodes[layer, 6 * m + c] for c in range(6)], axis=1)

    def around(result, c):
        even = result[0:GROUP, column(c)] + pltpu.roll(result[2 * GROUP :, column(c)], 1, axis=1)
        return even, result[GROUP : 2 * GROUP, column(c)]

    def points_of(layer, m, d):
        t_points[layer, m, d] = dot(ahead[4 * layer + d], stress_window(layer, m))

    def into(ref, values):
        for j in range(3):
            for i in range(3):
                ref[256 * j : 256 * j + POINTS, column(i)] = values[SLOT[i][j]]

    others = modes - 1 + has_below.astype(jnp.int32) + has_above.astype(jnp.int32)
    pl.semaphore_wait(barrier, others)

    @pl.when(has_below)
    def _():
        down_velocity.start()

    @pl.when(has_above)
    def _():
        up_velocity.start()

    @pl.when(has_below)
    def _():
        down_stress.start()

    arrived_here(4, 5, 6, 7)
    both = jnp.concatenate([stress_window(0, 0), stress_window(0, 1)], axis=0)
    upper = ahead[4].astype(F32)
    lane = lax.rem(lax.broadcasted_iota(jnp.int32, (POINTS, WINDOW), 1), OWN)
    zero = jnp.zeros_like(upper)
    parts = jnp.concatenate(
        [
            jnp.where(lane == 0, zero, upper).astype(BF16),
            jnp.where(lane == 0, upper, zero).astype(BF16),
            ahead[0],
        ],
        axis=0,
    )
    at = dot(jnp.concatenate([parts, parts], axis=1), both)
    for part in range(3):
        here = at[POINTS * part : POINTS * (part + 1)]
        if part == 1:
            here = here * inside
        here = here.astype(BF16)
        into(dflux.at[pl.ds(768 * part, 768)], [here[:, column(c)] for c in range(6)])
    outer = dot(back[1, :, 256:], dflux[0:768])
    for k in range(3):
        rows = slice(GROUP * k, GROUP * (k + 1))
        own = back[1, rows].astype(F32)
        zero = jnp.zeros_like(own)
        is_first = jnp.concatenate([first] * 8, axis=1)
        masked[0, rows] = jnp.where(is_first, own, zero)
        masked[1, rows] = jnp.where(is_first, zero, own[:, 0:1024])
    tested = jnp.concatenate([masked[0, :, 256:].astype(BF16), back[0, :, 256:]], axis=1)
    local = dot(tested, dflux[768:])
    cup_send[...] = raised(packed([jnp.concatenate(around(outer, i), axis=1) for i in range(3)]), SENT)

    @pl.when(has_above)
    def _():
        up_share.start()

    for i in range(3):
        even, odd = around(local, i)
        shares[GROUP * 2 * i : GROUP * (2 * i + 1)] = even
        shares[GROUP * (2 * i + 1) : GROUP * (2 * i + 2)] = odd

    def velocity_points(layer, at):
        at = at.astype(BF16).astype(F32)
        u = [at[:, column(i)] for i in range(3)]
        upwind = 0.5 / (1.0 + jnp.sqrt(u[0] * u[0] + u[1] * u[1] + u[2] * u[2]))
        for i in range(3):
            flow[layer, i] = u[i]
            winds[layer, i] = (upwind * u[i]).astype(BF16)

    def gradient_points(variant, layer):
        nodes = side(v_nodes, variant, 3)
        for j in range(3):
            at = dot(ahead[4 * layer + 1 + j], nodes)
            derivs[variant, 0:POINTS, 3 * LANES * j : 3 * LANES * (j + 1)] = at.astype(BF16)

    arrived_here(8)
    own_velocity = laid_out([raised(rows_of(velocity[i]), SENT) for i in range(3)])
    for i in range(3):
        v_nodes[0, i] = window(own_velocity[i])

    velocity_points(0, dot(ahead[0], side(v_nodes, 0, 3)))
    gradient_points(0, 0)

    @pl.when(has_above)
    def _():
        down_velocity.wait_recv()

    @pl.when(has_below)
    def _():
        up_velocity.wait_recv()

    two = [vel_below[k].astype(F32)[0:GROUP] for k in range(2)]
    six = laid_out(
        [raised(rows_of(vel_above[i]), SENT) for i in range(3)]
        + [raised(b, SENT) for b in (two[0], shifted(two[0], 2), two[1])]
    )
    higher, lower = six[0:3], six[3:6]
    own = [
        [v_nodes[0, i, 0:224].astype(F32)[GROUP * c : GROUP * (c + 1)] for c in range(3)]
        for i in range(3)
    ]
    for i in range(3):
        v_nodes[1, i] = window([jnp.where(first, higher[i][c], own[i][c]) for c in range(3)])
        v_nodes[2, i] = window([jnp.where(first, own[i][c] * inside, lower[i][c]) for c in range(3)])
        v_nodes[3, i] = window(higher[i])
    arrived_here(9)
    gradient_points(1, 1)
    gradient_points(2, 1)
    gradient_points(3, 0)
    tested = jnp.concatenate(
        [back[0, :, 0:256], masked[1, :, 0:256].astype(BF16), masked[0, :, 0:256].astype(BF16)], axis=1
    )
    grads[0] = dot(tested, jnp.concatenate([derivs[0], derivs[1], derivs[2]], axis=0))
    tested = jnp.concatenate([back[1, :, 0:256], back[0, :, 0:256]], axis=1)
    grads[1] = dot(tested, jnp.concatenate([derivs[1], derivs[3]], axis=0))

    @pl.when(has_above)
    def _():
        down_stress.wait_recv()

    higher = laid_out([str_above[g] for g in range(3)])
    for k in range(12):
        mine = s_nodes[0, k].astype(F32)
        s_nodes[1, k] = window(
            [
                jnp.where(
                    first, shifted(higher[k // 4][c], -(k % 4)), mine[GROUP * c : GROUP * (c + 1)]
                )
                for c in range(3)
            ]
        )
    both = jnp.concatenate([stress_window(1, 0), stress_window(1, 1)], axis=0)
    at = dot(jnp.concatenate([ahead[4], ahead[4]], axis=1), both).astype(BF16)
    into(dflux.at[pl.ds(0, 768)], [at[:, column(c)] for c in range(6)])
    upper = dot(back[1, :, 256:], dflux[0:768])

    @pl.when(has_below)
    def _():
        up_share.wait_recv()

    from_below = cup_recv[...].astype(F32)[0:GROUP]
    for i in range(3):
        even, odd = around(upper, i)
        arrived = shifted(from_below, -i)
        shares[GROUP * 2 * i : GROUP * (2 * i + 1)] += jnp.where(first, arrived[:, 0:LANES], even)
        shares[GROUP * (2 * i + 1) : GROUP * (2 * i + 2)] += jnp.where(first, arrived[:, LANES:], odd)
    for k in range(8):
        rs_send[k] = raised(shares[56 * k : 56 * (k + 1)], 64)

    def share_copy(off):
        peer = lax.rem(mode + off, modes)
        return remote(
            rs_send.at[peer], rs_recv.at[off], rs_ssem.at[off], rs_rsem.at[off], (dom, peer)
        )

    for off in range(1, modes):
        share_copy(off).start()

    arrived_here(10)
    start_mass = jnp.where(first, jnp.where(has_below, 1.0, 2.0).astype(F32), jnp.ones((GROUP, LANES), F32))
    end_mass = jnp.where(has_above, 1.0, 0.0).astype(F32)

    def project(j, _):
        for i in range(3):
            cols = pl.ds(pl.multiple_of((3 * j + i) * LANES, LANES), LANES)
            mine, over = [], []
            for c in range(3):
                rows = slice(GROUP * c, GROUP * (c + 1))
                mine.append(grads[0, rows, cols])
                over.append(grads[1, rows, cols])
            results = []
            for parts, scale in ((mine, start_mass), (over, end_mass)):
                even = (parts[0] + pltpu.roll(parts[2], 1, axis=1)) * (inv_mass[0] * scale)
                odd = parts[1] * (inv_mass[1] * scale)
                results.append([even, odd, pltpu.roll(even, LANES - 1, axis=1)])
            p_nodes[0, 3 * i + j] = window(results[0])
            p_nodes[1, 3 * i + j] = window(
                [jnp.where(first, results[1][c], results[0][c]) for c in range(3)]
            )
        return 0

    lax.fori_loop(0, 3, project, 0)

    def projected_points(layer):
        for i in range(3):
            nodes = jnp.concatenate([p_nodes[layer, 3 * i + j] for j in range(3)], axis=1)
            here = dot(ahead[4 * layer], nodes)
            for j in range(3):
                g_points[layer, 3 * i + j] = here[:, column(j)]

    projected_points(1)
    velocity_points(1, dot(ahead[4], side(v_nodes, 1, 3)))

    def residual_of(layer, m, following):
        lam = jnp.full((16, LANES), relax[2 * mode + m], F32)
        eta = jnp.full((16, LANES), viscosity[2 * mode + m], F32)
        eps = jnp.full((16, LANES), extension[2 * mode + m], F32)
        half = 0.5 / lam
        slope = 0.5 * eps / eta
        kappa = eta / lam

        def chunk(start):
            rows = pl.ds(start, 16)
            t = [t_points[layer, m, 0, rows, column(c)] for c in range(6)]
            g = [[g_points[layer, 3 * i + j, rows] for j in range(3)] for i in range(3)]
            u = [flow[layer, i, rows] for i in range(3)]
            y = half + slope * (t[0] + t[1] + t[2])
            shift = (y * kappa) * 2.0
            tt = [t[0] + kappa, t[1] + kappa, t[2] + kappa] + t[3:]
            h = [g[k][k] - y for k in range(3)]

            def entry(i, j):
                return tt[SLOT[i][j]]

            for c, (i, j) in enumerate(((0, 0), (1, 1), (2, 2), (0, 1), (0, 2), (1, 2))):
                value = u[0] * t_points[layer, m, 1, rows, column(c)]
                value = value + u[1] * t_points[layer, m, 2, rows, column(c)]
                value = value + u[2] * t_points[layer, m, 3, rows, column(c)]
                if i == j:
                    k, l = (i + 1) % 3, (i + 2) % 3
                    part = h[i] * entry(i, i) + g[i][k] * entry(k, i) + g[i][l] * entry(l, i)
                    value = value - (part + part) - shift
                else:
                    k = 3 - i - j
                    part = (h[i] + h[j]) * entry(i, j)
                    part = part + g[i][j] * entry(j, j) + g[i][k] * entry(k, j)
                    part = part + g[j][i] * entry(i, i) + g[j][k] * entry(k, i)
                    value = value - part
                rounded = value.astype(BF16)
                flux[rows, column(c)] = rounded
                for j2 in range(3):
                    place = pl.ds(256 * (1 + j2) + start, 16)
                    flux[place, column(c)] = rounded * winds[layer, j2, rows]

        def step(k, _):
            chunk(pl.multiple_of(16 * k, 16))
            return 0

        bounds = (0, 4, 8, 11, 14)
        for d in range(4):
            lax.fori_loop(bounds[d], bounds[d + 1], step, 0, unroll=True)
            if following is not None:
                points_of(*following, d)
        sums[layer, m] = dot(back[layer], flux[...])

    weight = viscosity[0]
    for k in range(1, 2 * modes):
        weight = weight + viscosity[k]
    weight = weight * (1.0 / (2 * modes))

    def devss_of(layer):
        values = [None] * 6
        for i in range(3):
            for j in range(i, 3):
                d_ij = derivs[layer, 0:POINTS, column(3 * j + i)].astype(F32)
                d_ji = derivs[layer, 0:POINTS, column(3 * i + j)].astype(F32)
                excess = d_ij + d_ji - g_points[layer, 3 * i + j] - g_points[layer, 3 * j + i]
                values[SLOT[i][j]] = (weight * excess).astype(BF16)
        into(dflux.at[pl.ds(0, 768)], values)
        devss[layer] = dot(back[layer, :, 256:], dflux[0:768])

    tops = [
        remote(top_send.at[k], top_recv.at[k], top_ssem.at[k], top_rsem.at[k], above) for k in range(4)
    ]

    for d in range(4):
        points_of(1, 0, d)
    devss_of(1)
    for m in range(2):
        residual_of(1, m, ((1, 1), (0, 0))[m])
        result = sums[1, m]
        blocks = [jnp.concatenate(around(result, c), axis=1) for c in range(6)]
        result = devss[1]
        for i in ((0, 1), (2,))[m]:
            blocks.append(jnp.concatenate(around(result, i), axis=1))
        top_send[2 * m] = raised(packed(blocks[0:4]), SENT)
        top_send[2 * m + 1] = raised(packed(blocks[4:]), SENT)

        @pl.when(has_above)
        def _():
            tops[2 * m].start()
            tops[2 * m + 1].start()

    def sum_shares():
        place = pl.ds(pl.multiple_of(mode * 56, 8), 56)
        total = jnp.concatenate([shares[place], jnp.zeros((8, LANES), F32)], axis=0)
        for off in range(1, modes):
            share_copy(off).wait_recv()
            total = total + rs_recv[off].astype(F32)
        ag_buf[mode] = total.astype(BF16)

    def whole_copy(off, place):
        peer = lax.rem(mode + off, modes)
        return remote(
            ag_buf.at[place], ag_buf.at[place], ag_ssem.at[off], ag_rsem.at[off], (dom, peer)
        )

    sum_shares()
    for off in range(1, modes):
        whole_copy(off, mode).start()

    projected_points(0)
    devss_of(0)
    for m in range(2):
        residual_of(0, m, ((0, 1), None)[m])

    @pl.when(has_below)
    def _():
        for k in range(4):
            tops[k].wait_recv()

    def nodes_of(lower, upper, c, arrived):
        parts = []
        for k in range(3):
            rows = slice(GROUP * k, GROUP * (k + 1))
            high = upper[rows, column(c)]
            parts.append(lower[rows, column(c)] + jnp.where(first, jnp.zeros_like(high), high))
        even = parts[0] + pltpu.roll(parts[2], 1, axis=1)
        both = jnp.concatenate([even, parts[1]], axis=1)
        return both + jnp.where(firsts, arrived, jnp.zeros_like(both))

    def finish(m, _):
        lam = relax[2 * mode + m]
        lower, upper = sums[0, m], sums[1, m]
        arrived = [top_recv[2 * m + k].astype(F32)[0:GROUP] for k in range(2)]
        for c in range(6):
            both = nodes_of(lower, upper, c, shifted(arrived[c // 4], -(c % 4)))
            pieces[6 * m + c] = raised(both * lam, SENT)
        return 0

    lax.fori_loop(0, 2, finish, 0)

    for off in range(1, modes):
        whole_copy(off, lax.rem(mode + modes - off, modes)).wait_recv()

    for k in range(8):
        shares[56 * k : 56 * (k + 1)] = ag_buf[k].astype(F32)[0:56]
    lower, upper = devss[0], devss[1]
    for i in range(3):
        group, place = ((1, 2), (1, 3), (3, 2))[i]
        arrived = shifted(top_recv[group].astype(F32)[0:GROUP], -place)
        both = nodes_of(lower, upper, i, arrived)
        both = both + jnp.concatenate(
            [
                shares[GROUP * 2 * i : GROUP * (2 * i + 1)],
                shares[GROUP * (2 * i + 1) : GROUP * (2 * i + 2)],
            ],
            axis=1,
        )
        rounded = both.astype(BF16).astype(F32)
        pieces[12 + i] = raised(rounded, SENT)
        pieces[15 + i] = raised(both - rounded, SENT)

    @pl.when(has_below)
    def _():
        down_velocity.wait_send()
        down_stress.wait_send()

    @pl.when(has_above)
    def _():
        up_velocity.wait_send()
        up_share.wait_send()
        for k in range(4):
            tops[k].wait_send()

    for off in range(1, modes):
        share_copy(off).wait_send()
        whole_copy(off, mode).wait_send()


def finish_kernel(pieces, merge, out_stress, out_div, stress_rows, div_rows, sem):
    def merged(first):
        rows = dot(jnp.concatenate([pieces[first + k] for k in range(3)], axis=0), merge[...])
        return [
            rows[SENT * k : SENT * k + OWN * NODES].reshape(NODES, OWN, 2 * LANES) for k in range(3)
        ]

    copies = []
    for g in range(4):
        place = (g // 2, pl.ds(3 * (g % 2), 3))
        for k, rows in enumerate(merged(3 * g)):
            stress_rows[g // 2, 3 * (g % 2) + k] = rows.astype(BF16)
        copies.append(pltpu.make_async_copy(stress_rows.at[place], out_stress.at[place], sem.at[g]))
        copies[g].start()
    for k, (high, low) in enumerate(zip(merged(12), merged(15))):
        div_rows[k] = high + low
    copies.append(pltpu.make_async_copy(div_rows, out_div, sem.at[4]))
    copies[4].start()
    for copy in copies:
        copy.wait()


def on_device(doms, modes, velocity, stress, relax_time, viscosity, extensibility):
    ahead, back = column_tables()
    split, merge = order_tables()
    velocity = jnp.transpose(velocity, (0, 2, 1, 3))
    stress = jnp.transpose(stress, (0, 1, 3, 2, 4))
    vmem = pl.BlockSpec(memory_space=pltpu.VMEM)
    smem = pl.BlockSpec(memory_space=pltpu.SMEM)
    hbm = pl.BlockSpec(memory_space=pltpu.HBM)
    dma = pltpu.SemaphoreType.DMA
    around_nodes = 2 * LANES
    scratch = [
        pltpu.VMEM(velocity.shape, BF16),
        pltpu.VMEM(stress.shape, BF16),
        pltpu.VMEM(ahead.shape, BF16),
        pltpu.VMEM(back.shape, BF16),
        pltpu.VMEM(split.shape, BF16),
        pltpu.VMEM((2, GROUP, LANES), F32),
        pltpu.VMEM((12, SENT, around_nodes), BF16),
        pltpu.VMEM((3, SENT, around_nodes), BF16),
        pltpu.VMEM((2, SENT, around_nodes), BF16),
        pltpu.VMEM(velocity.shape, BF16),
        pltpu.VMEM((2, SENT, around_nodes), BF16),
        pltpu.VMEM((3, SENT, around_nodes), BF16),
        pltpu.VMEM((SENT, around_nodes), BF16),
        pltpu.VMEM((SENT, around_nodes), BF16),
        pltpu.VMEM((4, SENT, around_nodes), BF16),
        pltpu.VMEM((4, SENT, around_nodes), BF16),
        pltpu.VMEM((2, 12, WINDOW, LANES), BF16),
        pltpu.VMEM((4, 3, WINDOW, LANES), BF16),
        pltpu.VMEM((2, 9, WINDOW, LANES), BF16),
        pltpu.VMEM((2, 2, 4, POINTS, 6 * LANES), F32),
        pltpu.VMEM((4 * 256, 6 * LANES), BF16),
        pltpu.VMEM((9 * 256, 3 * LANES), BF16),
        pltpu.VMEM((2, COLUMN, 4 * 256), F32),
        pltpu.VMEM((4, 256, 9 * LANES), BF16),
        pltpu.VMEM((2, COLUMN, 9 * LANES), F32),
        pltpu.VMEM((2, 3, POINTS, LANES), F32),
        pltpu.VMEM((2, 3, POINTS, LANES), BF16),
        pltpu.VMEM((2, 9, POINTS, LANES), F32),
        pltpu.VMEM((2, 2, COLUMN, 6 * LANES), F32),
        pltpu.VMEM((2, COLUMN, 3 * LANES), F32),
        pltpu.VMEM((448, LANES), F32),
        pltpu.VMEM((8, 64, LANES), BF16),
        pltpu.VMEM((8, 64, LANES), BF16),
        pltpu.VMEM((8, 64, LANES), BF16),
        dma((11,)),
        dma((4,)),
        dma((4,)),
        dma((modes,)),
        dma((modes,)),
        dma((modes,)),
        dma((modes,)),
        dma((4,)),
        dma((4,)),
    ]
    pieces = pl.pallas_call(
        functools.partial(kernel, doms, modes),
        out_shape=pltpu.VMEM((18, SENT, around_nodes), BF16),
        in_specs=[hbm, hbm, smem, smem, smem, hbm, hbm, hbm, hbm],
        out_specs=vmem,
        scratch_shapes=scratch,
        compiler_params=pltpu.CompilerParams(
            collective_id=0, has_side_effects=True, vmem_limit_bytes=58 * 1024 * 1024
        ),
        name="ptt",
    )(
        velocity,
        stress,
        relax_time,
        viscosity,
        extensibility,
        jnp.asarray(ahead),
        jnp.asarray(back),
        jnp.asarray(split),
        jnp.asarray(inverse_mass()),
    )
    out_stress, out_div = pl.pallas_call(
        finish_kernel,
        out_shape=(
            jax.ShapeDtypeStruct(stress.shape, BF16),
            jax.ShapeDtypeStruct(velocity.shape, F32),
        ),
        in_specs=[vmem, vmem],
        out_specs=(hbm, hbm),
        scratch_shapes=[pltpu.VMEM(stress.shape, BF16), pltpu.VMEM(velocity.shape, F32), dma((5,))],
        compiler_params=pltpu.CompilerParams(vmem_limit_bytes=16 * 1024 * 1024),
        name="finish",
    )(pieces, jnp.asarray(merge))
    return jnp.transpose(out_stress, (0, 1, 3, 2, 4)), jnp.transpose(out_div, (0, 2, 1, 3))


def solution(mesh):
    return jax.shard_map(
        functools.partial(on_device, mesh.shape["dom"], mesh.shape["mode"]),
        mesh=mesh,
        in_specs=(P(None, "dom", None, None), P("mode", None, "dom", None, None), P(), P(), P()),
        out_specs=(P("mode", None, "dom", None, None), P(None, "dom", None, None)),
        check_vma=False,
    )
```
